32 devices in a mesh: lat: 4 (over y, x), lon: 8 (over z, core).
Axes of the slice: x: 2, y: 2, z: 4, core: 2. Of those that a mesh axis runs over, the one named last changes fastest.
Arguments:
- background: bfloat16 [4, 8, 512, 1024], P('lat', 'lon'), may hold values from -6 to 6
- conv_pert: bfloat16 [4, 8, 128, 512], P('lat', 'lon'), may hold values from -6 to 6
- conv_misfit: bfloat16 [4, 8, 128], P('lat', 'lon'), may hold values from -6 to 6
- conv_column: int32 [4, 8, 128], P('lat', 'lon'), may hold values from 0 to 255
- sat_pert: bfloat16 [4, 128, 32, 512], P('lat', 'lon'), may hold values from -6 to 6
- sat_misfit: bfloat16 [4, 128, 32], P('lat', 'lon'), may hold values from -6 to 6
- sat_rows: int32 [4, 128], P('lat', 'lon'), may hold values from 1 to 32
- sat_targets: int32 [4, 128, 2], P('lat', 'lon'), may hold values from 0 to 7, all different within a row; in each aligned block of 16 rows (0 to 15, 16 to 31, ..., all dimensions but the last counted through in order) at most 8 rows name the same one
Outputs:
- analysis: float32 [4, 8, 512, 1024], P('lat', 'lon')
The draws below stay inside these ranges and needn't reach their ends.
Inputs may be any that keep to these rules, and one draw needn't show every extreme that they name: `sat_targets`: each tile names 2 different blocks. The tiles of one device name one block at most 8 times in all, and some device names some block exactly 8 times.
All inputs are finite; a program needn't handle non-finite values.
Results may differ from the reference program's by a relative error of at most 0.0073.
Values may be sent and summed in bfloat16 or wider, within the bound.
A program may use at most 128 MiB of HBM per device.

```python
import math
import jax
import jax.numpy as jnp
import numpy as np
from jax import lax

K = 512
BLK = 16
CONV = 128
TILES_DEV = 16
TILE_OBS = 32
LOC = 2
NS_ITERS = 3
COLS = 256
CELLS = 1024
TILES = 128
CAP = 8
N_LAT = 4
N_LON = 8


def draw_background(key, part):
    key = jax.random.fold_in(key, 3)
    values = jax.random.normal(key, (N_LAT, N_LON, K, CELLS), jnp.float32)
    return jnp.clip(values, -6.0, 6.0).astype(jnp.bfloat16)


def draw_conv_pert(key, part):
    key = jax.random.fold_in(key, 5)
    values = jax.random.normal(key, (N_LAT, N_LON, CONV, K), jnp.float32)
    return jnp.clip(values, -6.0, 6.0).astype(jnp.bfloat16)


def draw_sat_pert(key, part):
    key = jax.random.fold_in(key, 7)
    values = jax.random.normal(key, (N_LAT, TILES, TILE_OBS, K), jnp.float32)
    return jnp.clip(values, -6.0, 6.0).astype(jnp.bfloat16)


def touch_ends(array, own_key, least, top_value):
    place = [jax.random.randint(jax.random.fold_in(own_key, axis), (), 0, length) for axis, length in enumerate(array.shape)]
    longest = array.shape.index(max(array.shape))
    next_to = place[:longest] + [(place[longest] + 1) % array.shape[longest]] + place[longest + 1:]
    return array.at[tuple(place)].set(least).at[tuple(next_to)].set(top_value)


def block_levels(stream_key, dims, split, smallest, high):
    level, own = 1.0, jax.random.fold_in(stream_key, 6)
    for axis_at, shards_of in split:
        heights = jnp.exp(jax.random.uniform(jax.random.fold_in(own, axis_at), (shards_of,), jnp.float32, smallest / len(split), high / len(split)))
        level = level * jnp.repeat(heights, dims[axis_at] // shards_of).reshape([-1 if axis == axis_at else 1 for axis in range(len(dims))])
    return level


def deal_out(stream_key, own, number, rows, count, top, limit, lean):
    sequence = jax.random.permutation(stream_key, count)
    heavy_load, common = shares(count, rows * top, limit, lean, True), shares(count, rows * top, limit, lean, False)
    places = jnp.arange(count)

    def named(sizes, rotation):
        used = int((sizes > 0).sum())
        fixed = max(1, used // 4)
        moved = fixed + (places - fixed + rotation * (used - fixed)) % max(1, count - fixed)
        return jnp.zeros((count,), jnp.int32).at[sequence[jnp.where(places < fixed, places, moved)]].set(jnp.asarray(sizes, jnp.int32))

    sizes = jnp.where(number % 4 == 0, named(heavy_load, number // 4), named(common, number - number // 4 - 1))
    mixed = jax.random.permutation(jax.random.fold_in(own, 3), count)
    source_of, sink = mixed[0:count // 2 * 2:2], mixed[1:count // 2 * 2:2]
    slack = jnp.minimum(sizes[source_of] - 1, limit - sizes[sink]) // 2
    slack = jnp.where((source_of == sequence[0]) | (sink == sequence[0]) | (sizes[sink] == 0), 0, jnp.maximum(slack, 0))
    moved = jax.random.randint(jax.random.fold_in(own, 4), (count // 2,), 0, 1 << 20) % (slack + 1)
    sizes = sizes.at[source_of].add(-moved).at[sink].add(moved)
    items = jnp.searchsorted(jnp.cumsum(sizes), jnp.arange(rows * top), side="right").astype(jnp.int32)
    grid = items.reshape(top, rows).T
    grid = grid[jax.random.permutation(jax.random.fold_in(own, 1), rows)]
    rotation = jax.random.randint(jax.random.fold_in(own, 2), (rows, 1), 0, top)
    return jnp.take_along_axis(grid, (jnp.arange(top)[None, :] + rotation) % top, axis=1)


def shares(amount, total, limit, lean, full):
    weights = [(1 << 20) // math.isqrt(standing ** lean) + 1 for standing in range(1, amount + 1)]
    largest = limit if full else min(limit, max(-(-total // amount), total * weights[0] // sum(weights)))
    least = 1 if total - largest >= amount - 1 else 0
    holding, spare = [largest] + [least] * (amount - 1), total - largest - least * (amount - 1)
    while spare > 0:
        movable = [i for i in range(1, amount) if holding[i] < largest] or [i for i in range(1, amount) if holding[i] < limit]
        pool, budget = sum([weights[i] for i in movable]), spare
        for i in movable:
            addition = min(limit - holding[i], max(1, budget * weights[i] // pool), spare)
            holding[i] = holding[i] + addition
            spare = spare - addition
    return np.array(holding)


def normal_values(own_key, shape, scale, reach, split=(), kind=jnp.bfloat16):
    values = scale * jax.random.normal(own_key, shape, jnp.float32)
    if split:
        values = values * block_levels(own_key, shape, split, -0.22, 0.18)
    return jnp.clip(values, -reach, reach).astype(kind)


def setup_inputs(seed: int = 0) -> dict:
    arg_keys = jax.random.split(jax.random.key(seed), 9)
    background = draw_background(jax.random.fold_in(arg_keys[8], 71), 0)
    conv_pert = draw_conv_pert(jax.random.fold_in(arg_keys[8], 71), 0)
    conv_misfit = normal_values(arg_keys[2], (N_LAT, N_LON, CONV), 1.0, 6.0, ((0, 4), (1, 8)))
    conv_column = touch_ends(jax.random.randint(arg_keys[3], (N_LAT, N_LON, CONV), 0, COLS), jax.random.fold_in(arg_keys[3], 1), 0, COLS - 1).astype(jnp.int32)
    sat_pert = draw_sat_pert(jax.random.fold_in(arg_keys[8], 71), 0)
    sat_misfit = normal_values(arg_keys[5], (N_LAT, TILES, TILE_OBS), 1.0, 6.0, ((0, 4), (1, 8)))
    sat_rows = touch_ends(jax.random.randint(arg_keys[6], (N_LAT, TILES), 1, TILE_OBS + 1), jax.random.fold_in(arg_keys[6], 1), 1, TILE_OBS).astype(jnp.int32)
    sat_targets_keys = jax.random.split(jax.random.fold_in(arg_keys[7], 1), N_LAT * TILES // TILES_DEV)
    sat_targets_turns = jax.random.permutation(jax.random.fold_in(arg_keys[7], 3), N_LAT * TILES // TILES_DEV)
    sat_targets = jax.vmap(lambda own, number: deal_out(jax.random.fold_in(arg_keys[7], 2), own, number, TILES_DEV, N_LON, LOC, CAP, 2))(sat_targets_keys, sat_targets_turns).reshape((N_LAT, TILES, LOC))
    return {"background": background, "conv_pert": conv_pert, "conv_misfit": conv_misfit, "conv_column": conv_column, "sat_pert": sat_pert, "sat_misfit": sat_misfit, "sat_rows": sat_rows, "sat_targets": sat_targets}


def local_weight(column, lat_shift, lon_shift):
    lat_place = BLK * lat_shift + (column // BLK).astype(jnp.float32) + 0.5 - 0.5 * BLK
    lon_place = BLK * lon_shift + (column % BLK).astype(jnp.float32) + 0.5 - 0.5 * BLK
    return jnp.exp(-(lat_place * lat_place + lon_place * lon_place) / (2.0 * BLK * BLK))

def analyse(gram_sum, drive_sum, ensemble):
    members = ensemble.shape[0]
    highest = lax.Precision.HIGHEST
    identity = jnp.eye(members, dtype=jnp.float32)
    system = (members - 1.0) * identity + gram_sum
    scale = jnp.sqrt(jnp.sum(system * system))
    iterate = system / scale
    inverse_root = identity
    for sweep_index in range(NS_ITERS):
        middle = 1.5 * identity - 0.5 * jnp.dot(inverse_root, iterate, precision=highest)
        iterate = jnp.dot(iterate, middle, precision=highest)
        inverse_root = jnp.dot(middle, inverse_root, precision=highest)
    covariance = jnp.dot(inverse_root, inverse_root, precision=highest) / scale
    mean_weight = jnp.dot(covariance, drive_sum, precision=highest)
    transform = (jnp.sqrt((members - 1.0) / scale) * inverse_root + mean_weight[:, None]).astype(jnp.bfloat16)
    state_mean = lax.optimization_barrier(jnp.mean(ensemble.astype(jnp.float32), axis=0))
    anomaly = (ensemble.astype(jnp.float32) - state_mean).astype(jnp.bfloat16)
    return state_mean + lax.dot_general(transform, anomaly, (((0,), (0,)), ((), ())), preferred_element_type=jnp.float32)

def shift_blocks(values, lat_shift, lon_shift):
    rolled = jnp.roll(values, -lon_shift, axis=1)
    widths = [(1, 1)] + [(0, 0)] * (values.ndim - 1)
    padded = jnp.pad(rolled, widths)
    return padded[1 + lat_shift:1 + lat_shift + values.shape[0]]

def reference(background, conv_pert, conv_misfit, conv_column, sat_pert, sat_misfit, sat_rows, sat_targets):
    tile_total = TILES_DEV * N_LON
    entry_weight = 0.5 ** jnp.arange(LOC).astype(jnp.float32)
    obs_index = jnp.arange(TILE_OBS).astype(jnp.int32)

    def add_tile(tile_number, totals):
        gram_all, drive_all = totals
        band_index = tile_number // tile_total
        tile_slot = tile_number % tile_total
        spread = sat_pert[band_index, tile_slot]
        misfit = sat_misfit[band_index, tile_slot]
        live = obs_index < sat_rows[band_index, tile_slot]
        for list_slot in range(LOC):
            target = sat_targets[band_index, tile_slot, list_slot]
            keep_rows = jnp.where(live, entry_weight[list_slot], 0.0)
            scaled = (keep_rows[:, None] * spread).astype(jnp.bfloat16)
            gram_all = gram_all.at[band_index, target].add(jnp.dot(scaled.T, spread, preferred_element_type=jnp.float32))
            drive_all = drive_all.at[band_index, target].add(jnp.dot(misfit, scaled, preferred_element_type=jnp.float32))
        return (gram_all, drive_all)
    gram_all = jnp.zeros((N_LAT, N_LON, K, K), jnp.float32)
    drive_all = jnp.zeros((N_LAT, N_LON, K), jnp.float32)
    gram_all, drive_all = lax.fori_loop(0, N_LAT * tile_total, add_tile, (gram_all, drive_all))
    for lat_shift in (-1, 0, 1):
        for lon_shift in (-1, 0, 1):
            spread = shift_blocks(conv_pert, lat_shift, lon_shift)
            misfit = shift_blocks(conv_misfit, lat_shift, lon_shift)
            column = shift_blocks(conv_column, lat_shift, lon_shift)
            weight = local_weight(column, lat_shift, lon_shift)
            scaled = (weight[..., None] * spread).astype(jnp.bfloat16)
            gram_all = gram_all + jnp.einsum('abok,abol->abkl', scaled.astype(jnp.float32), spread.astype(jnp.float32))
            drive_all = drive_all + jnp.einsum('abok,abo->abk', scaled.astype(jnp.float32), misfit.astype(jnp.float32))
    flat = (gram_all.reshape(-1, K, K), drive_all.reshape(-1, K), background.reshape(-1, K, CELLS))
    result = lax.map(lambda block_items: analyse(*block_items), flat)
    return result.reshape(N_LAT, N_LON, K, CELLS)
```

```python
import functools

import jax
import jax.numpy as jnp
from jax import lax
from jax.experimental import pallas as pl
from jax.experimental.pallas import tpu as pltpu
from jax.sharding import PartitionSpec as P

BLK = 16
MESH = pl.DeviceIdType.MESH
F32 = jnp.float32
BF16 = jnp.bfloat16
EXTRA = 16


def dot(left, right):
    return lax.dot_general(left, right, (((1,), (0,)), ((), ())), preferred_element_type=F32)


def iota(shape, dim):
    return lax.broadcasted_iota(jnp.int32, shape, dim)


def gather_kernel(
    n_lat, n_lon,
    conv_pert, conv_misfit, conv_column, sat_pert, sat_misfit, sat_rows, sat_targets,
    out,
    sat_buf, conv_buf, sat_flip, conv_flip, acc, send_buf, recv_buf,
    sat_send, sat_recv, conv_send, conv_recv, line_send, line_recv,
):
    chips = n_lon // 2
    band = lax.axis_index("lat")
    block = lax.axis_index("lon")
    chip, core = block // 2, block % 2
    sibling = 2 * chip + (1 - core)
    tiles, tile_obs = sat_misfit.shape[1], sat_misfit.shape[2]
    rows, members = tiles * tile_obs, sat_pert.shape[3]
    conv_obs = conv_pert.shape[2]
    half = members // 2
    has_north, has_south = band > 0, band < n_lat - 1
    has_low, has_high = chip > 0, chip < chips - 1
    mates = (
        (has_north, (band - 1, block)),
        (has_south, (band + 1, block)),
        (has_low, (band, block - 2)),
        (has_high, (band, block + 2)),
    )

    conv_buf[0, 1, :conv_obs, :] = conv_pert[0, 0]
    conv_buf[0, 1, conv_obs:, :] = jnp.concatenate(
        [
            jnp.broadcast_to(conv_column[0].astype(F32).astype(BF16), (EXTRA, conv_obs)),
            jnp.broadcast_to(conv_misfit[0], (EXTRA, conv_obs)),
            jnp.zeros((EXTRA, members - 2 * conv_obs), BF16),
        ],
        axis=1,
    )

    own_tile = iota((tiles, rows), 1) // tile_obs == iota((tiles, rows), 0)
    spread_obs = (iota((tile_obs, rows), 1) % tile_obs == iota((tile_obs, rows), 0)).astype(BF16)
    misfit = jnp.sum(jnp.where(own_tile, dot(sat_misfit[0], spread_obs), 0.0), axis=0, keepdims=True)
    count = dot(
        jnp.broadcast_to(sat_rows[...].astype(F32).astype(BF16), (8, tiles)), own_tile.astype(BF16)
    )[0:1]
    live = (iota((1, rows), 1) % tile_obs).astype(F32) < count
    names = sat_targets[0].astype(F32)
    lists = [
        jnp.where(
            live,
            jnp.sum(jnp.where(own_tile, names[:, e : e + 1], 0.0), axis=0, keepdims=True),
            -1.0,
        )
        for e in range(2)
    ]
    place = iota((EXTRA, rows), 0)
    sat_buf[0, :rows, :] = sat_pert[0].reshape(rows, members)
    sat_buf[0, rows:, :] = jnp.where(
        place == 0, lists[0], jnp.where(place == 1, lists[1], jnp.where(place == 2, misfit, 0.0))
    ).astype(BF16)

    barrier = pltpu.get_barrier_semaphore()
    pl.semaphore_signal(barrier, inc=1, device_id=(band, sibling), device_id_type=MESH)
    for here, mate in mates:
        @pl.when(here)
        def _():
            pl.semaphore_signal(barrier, inc=1, device_id=mate, device_id_type=MESH)
    pl.semaphore_wait(barrier, 1 + sum(here.astype(jnp.int32) for here, _ in mates))

    sat_copy = pltpu.make_async_remote_copy(
        src_ref=sat_buf.at[0], dst_ref=sat_buf.at[1], send_sem=sat_send, recv_sem=sat_recv,
        device_id=(band, sibling), device_id_type=MESH,
    )
    sat_copy.start()

    def conv_copy(group, slot, to_group, to_slot, sem, mate):
        return pltpu.make_async_remote_copy(
            src_ref=conv_buf.at[group, slot], dst_ref=conv_buf.at[to_group, to_slot],
            send_sem=conv_send.at[sem], recv_sem=conv_recv.at[sem],
            device_id=mate, device_id_type=MESH,
        )

    to_north = conv_copy(0, 1, 0, 2, 0, (band - 1, block))
    to_south = conv_copy(0, 1, 0, 0, 1, (band + 1, block))
    to_side = conv_copy(0, 1, 1, 1, 2, (band, sibling))
    relays = [conv_copy(0, 0, 1, 0, 3, (band, sibling)), conv_copy(0, 2, 1, 2, 4, (band, sibling))]
    blank = jnp.zeros((conv_obs + EXTRA, members), BF16)

    @pl.when(has_north)
    def _():
        to_north.start()

    @pl.when(has_south)
    def _():
        to_south.start()

    to_side.start()

    @pl.when(jnp.logical_not(has_north))
    def _():
        conv_buf[0, 0] = blank
        conv_buf[1, 0] = blank

    @pl.when(jnp.logical_not(has_south))
    def _():
        conv_buf[0, 2] = blank
        conv_buf[1, 2] = blank

    def flip_sat(side):
        sat_flip[:, pl.ds(side * rows, rows)] = sat_buf[side, :rows, :].T

    flip_sat(0)
    sat_copy.wait_recv()
    flip_sat(1)

    def relay():
        @pl.when(has_north)
        def _():
            to_south.wait_recv()
            relays[0].start()

        @pl.when(has_south)
        def _():
            to_north.wait_recv()
            relays[1].start()

    def conv_ready():
        to_side.wait_recv()

        @pl.when(has_north)
        def _():
            relays[0].wait_recv()

        @pl.when(has_south)
        def _():
            relays[1].wait_recv()

        for group in range(2):
            for slot in range(3):
                at = (group * 3 + slot) * conv_obs
                conv_flip[:, at : at + conv_obs] = conv_buf[group, slot, :conv_obs, :].T

    def conv_weight(group, slot, target):
        column = conv_buf[group, slot, conv_obs:, :conv_obs][0:1].astype(F32)
        source = block if group == 0 else sibling
        away = lax.rem(source - target + 1 + n_lon, n_lon) - 1
        row = jnp.floor(column * (1.0 / BLK))
        lat_place = BLK * (slot - 1.0) + row + 0.5 - 0.5 * BLK
        lon_place = BLK * away.astype(F32) + (column - BLK * row) + 0.5 - 0.5 * BLK
        weight = jnp.exp(-(lat_place * lat_place + lon_place * lon_place) / (2.0 * BLK * BLK))
        return jnp.where(away <= 1, weight, 0.0)

    place = iota((EXTRA, members), 0)
    eye = iota((half, half), 0) == iota((half, half), 1)
    upper = iota((half, half), 0) <= iota((half, half), 1)

    def add_terms(slot, scaled, spread, forced, first):
        top = dot(scaled[:half], spread)
        low = dot(scaled[half:], spread[:, half:])
        drive = dot(forced, spread)
        diagonal = jnp.sum(jnp.where(eye, low, 0.0), axis=0, keepdims=True)
        packed = jnp.where(upper, top[:, :half], low)
        tail = jnp.where(place == 0, drive[0:1], 0.0) + jnp.where(
            place == 2, jnp.concatenate([diagonal, jnp.zeros_like(diagonal)], axis=1), 0.0
        )
        if first:
            acc[slot, :half, :half] = packed
            acc[slot, :half, half:] = top[:, half:]
            acc[slot, half:, :] = tail
        else:
            acc[slot, :half, :half] += packed
            acc[slot, :half, half:] += top[:, half:]
            acc[slot, half:, :] += tail

    def compute(slot, to_chip):
        target = 2 * to_chip + core
        name = target.astype(F32)

        weights, pushes = [], []
        for side in range(2):
            lists = sat_buf[side, rows:, :].astype(F32)
            weight = jnp.where(lists[0:1] == name, 1.0, 0.0) + jnp.where(lists[1:2] == name, 0.5, 0.0)
            weights.append(weight)
            pushes.append(weight * lists[2:3])
        weight = jnp.concatenate(weights, axis=1)
        push = jnp.concatenate(pushes, axis=1)
        scaled = sat_flip[...] * weight.astype(BF16)
        spread = jnp.concatenate([sat_buf[side, :rows, :] for side in range(2)], axis=0)
        add_terms(slot, scaled, spread, jnp.broadcast_to(push, (EXTRA, 2 * rows)).astype(BF16), True)

        near = jnp.logical_or(to_chip == chip, to_chip == wrapped)

        @pl.when(near)
        def _():
            weights, pushes, spreads = [], [], []
            for group in range(2):
                for place in range(3):
                    weight = conv_weight(group, place, target)
                    misfit = conv_buf[group, place, conv_obs:, conv_obs : 2 * conv_obs][0:1].astype(F32)
                    weights.append(weight)
                    pushes.append(weight * misfit)
                    spreads.append(conv_buf[group, place, :conv_obs, :])
            weight = jnp.concatenate(weights, axis=1)
            push = jnp.concatenate(pushes, axis=1)
            push_high = push.astype(BF16)
            scaled = (conv_flip[...].astype(F32) * weight).astype(BF16)
            spread = jnp.concatenate(spreads, axis=0)
            add_terms(slot, scaled, spread, jnp.broadcast_to(push_high, (EXTRA, 6 * conv_obs)), False)

    def line_copy(way, to_chip):
        ahead = block + 2 if way == 0 else block - 2
        return pltpu.make_async_remote_copy(
            src_ref=send_buf.at[way, to_chip], dst_ref=recv_buf.at[way, to_chip],
            send_sem=line_send.at[way, to_chip], recv_sem=line_recv.at[way, to_chip],
            device_id=(band, ahead), device_id_type=MESH,
        )

    def step_of(way, step):
        if way == 0:
            to_chip = chips - 1 + chip - step
            return to_chip, jnp.logical_and(to_chip > chip, to_chip < chips), has_low
        to_chip = step + chip - chips + 1
        return to_chip, jnp.logical_and(to_chip >= 0, to_chip < chip), has_high

    def finish(way, slot, to_chip, behind):
        @pl.when(behind)
        def _():
            line_copy(way, to_chip).wait_recv()
            acc[slot] += recv_buf[way, to_chip].astype(F32)

        value = acc[slot]
        tail = value[half:]
        high = tail[0:1].astype(BF16).astype(F32)
        kept = tail[2:3].astype(BF16).astype(F32)
        send_buf[way, to_chip, :half, :] = value[:half].astype(BF16)
        send_buf[way, to_chip, half:, :] = jnp.where(
            place == 1,
            tail[0:1] + tail[1:2] - high,
            jnp.where(place == 3, tail[2:3] + tail[3:4] - kept, tail),
        ).astype(BF16)
        line_copy(way, to_chip).start()

    def step_body(step, carry):
        for way in range(2):
            to_chip, wanted, behind = step_of(way, step)

            @pl.when(wanted)
            def _():
                @pl.when(to_chip == wrapped)
                def _():
                    conv_ready()

                compute(way, to_chip)
        for way in range(2):
            to_chip, wanted, behind = step_of(way, step)

            @pl.when(wanted)
            def _():
                finish(way, way, to_chip, behind)

        @pl.when(jnp.logical_and(step == 0, jnp.logical_not(early)))
        def _():
            relay()

        return carry

    wrapped = lax.rem(chip + 1 - 2 * core + chips, chips)
    early = jnp.logical_or(
        jnp.logical_and(jnp.logical_not(has_low), wrapped == chips - 1),
        jnp.logical_and(jnp.logical_not(has_high), wrapped == 0),
    )

    @pl.when(early)
    def _():
        relay()

    lax.fori_loop(0, chips - 1, step_body, 0)

    compute(0, chip)

    @pl.when(has_low)
    def _():
        line_copy(0, chip).wait_recv()
        acc[0] += recv_buf[0, chip].astype(F32)

    @pl.when(has_high)
    def _():
        line_copy(1, chip).wait_recv()
        acc[0] += recv_buf[1, chip].astype(F32)

    out[...] = acc[0]

    sat_copy.wait_send()
    to_side.wait_send()

    @pl.when(has_north)
    def _():
        to_north.wait_send()
        relays[0].wait_send()

    @pl.when(has_south)
    def _():
        to_south.wait_send()
        relays[1].wait_send()

    def drain(step, carry):
        for way in range(2):
            to_chip, wanted, _ = step_of(way, step)

            @pl.when(wanted)
            def _():
                line_copy(way, to_chip).wait_send()
        return carry

    lax.fori_loop(0, chips - 1, drain, 0)


def analyse_kernel(packed, background, out):
    members = background.shape[2]
    half = members // 2
    field = packed[:half, :half]
    cross = packed[:half, half:]
    drive = packed[half : half + 1] + packed[half + 1 : half + 2]
    diagonal = (packed[half + 2 : half + 3] + packed[half + 3 : half + 4])[:, :half]
    row, col = iota((half, half), 0), iota((half, half), 1)
    strict = jnp.where(row < col, field, 0.0)
    under = jnp.where(row > col, field, 0.0)
    first = jnp.where(row <= col, field, 0.0) + strict.T
    second = under + under.T + jnp.where(row == col, diagonal, 0.0)
    gram = jnp.concatenate(
        [jnp.concatenate([first, cross], axis=1), jnp.concatenate([cross.T, second], axis=1)], axis=0
    )
    one = (iota((members, members), 0) == iota((members, members), 1)).astype(F32)
    system = (members - 1.0) * one + gram
    scale = jnp.sqrt(jnp.sum(jnp.sum(system * system, axis=0, keepdims=True), axis=1, keepdims=True))
    y = system / scale
    yb = y.astype(BF16)
    square = dot(yb, yb)
    u = 1.5 * y - 0.5 * square
    w = 0.25 * square - 1.5 * y
    q = 2.25 * u + dot(u.astype(BF16), w.astype(BF16))
    e2 = -0.75 * y - 0.5 * q
    e2b = e2.astype(BF16)
    f = 2.25 * y + dot(yb, e2b)
    h = 4.5 * e2 + dot(e2b, e2b)
    e3 = 1.5 * e2 - 0.5 * (5.0625 * f + dot(f.astype(BF16), h.astype(BF16)))
    e3b = e3.astype(BF16)

    def times_root(vector):
        high = vector.astype(BF16)
        low = (vector - high.astype(F32)).astype(BF16)
        place = iota((16, members), 0)
        both = jnp.where(place == 0, high.astype(F32), jnp.where(place == 1, low.astype(F32), 0.0))
        product = dot(both.astype(BF16), e3b)
        return 3.375 * vector + product[0:1] + product[1:2]

    mean_weight = times_root(times_root(drive)) / scale
    transform = (jnp.sqrt((members - 1.0) / scale) * (3.375 * one + e3)).astype(BF16)

    ensemble = background[0, 0].astype(F32)
    state_mean = jnp.mean(ensemble, axis=0, keepdims=True)
    anomaly = (ensemble - state_mean).astype(BF16)
    high = mean_weight.astype(BF16)
    low = (mean_weight - high.astype(F32)).astype(BF16)
    place = iota((16, members), 0)
    both = jnp.where(place == 0, high.astype(F32), jnp.where(place == 1, low.astype(F32), 0.0))
    shift = dot(both.astype(BF16), anomaly)
    out[0, 0] = dot(transform, anomaly) + (state_mean + shift[0:1] + shift[1:2])


def shards(
    n_lat, n_lon,
    background, conv_pert, conv_misfit, conv_column, sat_pert, sat_misfit, sat_rows, sat_targets,
):
    members, cells = background.shape[2:]
    tiles, tile_obs = sat_pert.shape[1:3]
    conv_obs = conv_pert.shape[2]
    rows, chips, half = tiles * tile_obs, n_lon // 2, members // 2
    vmem = pl.BlockSpec(memory_space=pltpu.VMEM)
    packed = pl.pallas_call(
        functools.partial(gather_kernel, n_lat, n_lon),
        out_shape=jax.ShapeDtypeStruct((half + EXTRA, members), F32),
        in_specs=[vmem] * 7,
        out_specs=vmem,
        scratch_shapes=[
            pltpu.VMEM((2, rows + EXTRA, members), BF16),
            pltpu.VMEM((2, 3, conv_obs + EXTRA, members), BF16),
            pltpu.VMEM((members, 2 * rows), BF16),
            pltpu.VMEM((members, 6 * conv_obs), BF16),
            pltpu.VMEM((2, half + EXTRA, members), F32),
            pltpu.VMEM((2, chips, half + EXTRA, members), BF16),
            pltpu.VMEM((2, chips, half + EXTRA, members), BF16),
            pltpu.SemaphoreType.DMA,
            pltpu.SemaphoreType.DMA,
            pltpu.SemaphoreType.DMA((5,)),
            pltpu.SemaphoreType.DMA((5,)),
            pltpu.SemaphoreType.DMA((2, chips)),
            pltpu.SemaphoreType.DMA((2, chips)),
        ],
        compiler_params=pltpu.CompilerParams(
            collective_id=0, has_side_effects=True, vmem_limit_bytes=48 * 1024 * 1024
        ),
        cost_estimate=pl.CostEstimate(
            flops=2 * (chips * 2 * rows + 9 * conv_obs) * members * members,
            bytes_accessed=4 * rows * members, transcendentals=0,
        ),
        name="gather_grams",
    )(conv_pert, conv_misfit, conv_column, sat_pert, sat_misfit, sat_rows, sat_targets)
    return pl.pallas_call(
        analyse_kernel,
        out_shape=jax.ShapeDtypeStruct((1, 1, members, cells), F32),
        in_specs=[vmem] * 2,
        out_specs=vmem,
        compiler_params=pltpu.CompilerParams(vmem_limit_bytes=48 * 1024 * 1024),
        cost_estimate=pl.CostEstimate(
            flops=14 * members * members * members, bytes_accessed=6 * members * cells, transcendentals=0
        ),
        name="analyse",
    )(packed, background)


def solution(mesh):
    placed = (
        P("lat", "lon", None, None),
        P("lat", "lon", None, None),
        P("lat", "lon", None),
        P("lat", "lon", None),
        P("lat", "lon", None, None),
        P("lat", "lon", None),
        P("lat", "lon"),
        P("lat", "lon", None),
    )
    return jax.shard_map(
        functools.partial(shards, mesh.shape["lat"], mesh.shape["lon"]),
        mesh=mesh, in_specs=placed, out_specs=P("lat", "lon", None, None), check_vma=False,
    )
```

```python
import functools

import jax
import jax.numpy as jnp
from jax import lax
from jax.experimental import pallas as pl
from jax.experimental.pallas import tpu as pltpu
from jax.sharding import PartitionSpec as P

BLK = 16
MESH = pl.DeviceIdType.MESH
F32 = jnp.float32
BF16 = jnp.bfloat16
EXTRA = 16
LANES = 128
STORES = 4


def dot(left, right):
    return lax.dot_general(left, right, (((1,), (0,)), ((), ())), preferred_element_type=F32)


def iota(shape, dim):
    return lax.broadcasted_iota(jnp.int32, shape, dim)


def gather_kernel(
    n_lat, n_lon,
    conv_pert, conv_misfit, conv_column, sat_pert, sat_misfit, sat_rows, sat_targets,
    out,
    small_misfit, small_column, tile_misfit, tile_rows, tile_targets,
    sat_buf, sat_lists, conv_buf, sat_flip, conv_flip, acc, send_buf, recv_buf,
    load, sat_send, sat_recv, conv_send, conv_recv, line_send, line_recv,
):
    chips = n_lon // 2
    band = lax.axis_index("lat")
    block = lax.axis_index("lon")
    chip, core = block // 2, block % 2
    sibling = 2 * chip + (1 - core)
    opposite = n_lon - 1 - block
    tiles, tile_obs = sat_misfit.shape[1], sat_misfit.shape[2]
    rows, members = tiles * tile_obs, sat_pert.shape[1]
    conv_obs = conv_pert.shape[2]
    half, lane_blocks = members // 2, members // LANES
    has_north, has_south = band > 0, band < n_lat - 1
    has_low, has_high = chip > 0, chip < chips - 1
    outer = jnp.logical_or(block == 0, block == n_lon - 1)
    mates = (
        (has_north, (band - 1, block)),
        (has_south, (band + 1, block)),
        (has_low, (band, block - 2)),
        (has_high, (band, block + 2)),
        (outer, (band, opposite)),
    )

    barrier = pltpu.get_barrier_semaphore()
    pl.semaphore_signal(barrier, inc=1, device_id=(band, sibling), device_id_type=MESH)
    for here, mate in mates:
        @pl.when(here)
        def _():
            pl.semaphore_signal(barrier, inc=1, device_id=mate, device_id_type=MESH)

    loads = [
        pltpu.make_async_copy(source, target, load.at[at])
        for at, (source, target) in enumerate(
            (
                (conv_pert.at[0, 0], conv_buf.at[0, 1, pl.ds(0, conv_obs)]),
                (conv_misfit, small_misfit),
                (conv_column, small_column),
                (sat_misfit, tile_misfit),
                (sat_rows, tile_rows),
                (sat_targets, tile_targets),
                (sat_pert, sat_buf.at[0]),
            )
        )
    ]
    for copy in loads:
        copy.start()
    pl.semaphore_wait(barrier, 1 + sum(here.astype(jnp.int32) for here, _ in mates))

    def sat_copy(source, target, at):
        return pltpu.make_async_remote_copy(
            src_ref=source, dst_ref=target, send_sem=sat_send.at[at], recv_sem=sat_recv.at[at],
            device_id=(band, sibling), device_id_type=MESH,
        )

    tile_copy = sat_copy(sat_pert, sat_buf.at[1], 0)
    list_copy = sat_copy(sat_lists.at[0], sat_lists.at[1], 1)
    tile_copy.start()

    for copy in loads[:6]:
        copy.wait()
    conv_buf[0, 1, conv_obs:, :] = jnp.concatenate(
        [
            jnp.broadcast_to(small_column[0].astype(F32).astype(BF16), (EXTRA, conv_obs)),
            jnp.broadcast_to(small_misfit[0], (EXTRA, conv_obs)),
            jnp.zeros((EXTRA, members - 2 * conv_obs), BF16),
        ],
        axis=1,
    )

    def conv_copy(group, slot, to_group, to_slot, sem, mate):
        return pltpu.make_async_remote_copy(
            src_ref=conv_buf.at[group, slot], dst_ref=conv_buf.at[to_group, to_slot],
            send_sem=conv_send.at[sem], recv_sem=conv_recv.at[sem],
            device_id=mate, device_id_type=MESH,
        )

    to_north = conv_copy(0, 1, 0, 2, 0, (band - 1, block))
    to_south = conv_copy(0, 1, 0, 0, 1, (band + 1, block))
    to_side = conv_copy(0, 1, 1, 1, 2, (band, sibling))
    relays = [conv_copy(0, 0, 1, 0, 3, (band, sibling)), conv_copy(0, 2, 1, 2, 4, (band, sibling))]
    around = conv_copy(0, 1, 2, 1, 5, (band, opposite))
    far_north = conv_copy(2, 1, 2, 2, 6, (band - 1, block))
    far_south = conv_copy(2, 1, 2, 0, 7, (band + 1, block))

    @pl.when(outer)
    def _():
        around.start()

    @pl.when(has_north)
    def _():
        to_north.start()

    @pl.when(has_south)
    def _():
        to_south.start()

    own_tile = iota((tiles, rows), 1) // tile_obs == iota((tiles, rows), 0)
    own_mask = own_tile.astype(BF16)
    spread_obs = (iota((tile_obs, rows), 1) % tile_obs == iota((tile_obs, rows), 0)).astype(BF16)
    misfit = jnp.sum(jnp.where(own_tile, dot(tile_misfit[0], spread_obs), 0.0), axis=0, keepdims=True)
    count = dot(jnp.broadcast_to(tile_rows[...].astype(F32).astype(BF16), (8, tiles)), own_mask)[0:1]
    live = (iota((1, rows), 1) % tile_obs).astype(F32) < count
    names = tile_targets[0].astype(F32)
    lists = [
        jnp.where(
            live,
            dot(jnp.broadcast_to(names[e : e + 1], (8, tiles)).astype(BF16), own_mask)[0:1],
            -1.0,
        )
        for e in range(2)
    ]
    place = iota((EXTRA, rows), 0)
    sat_lists[0] = jnp.where(
        place == 0, lists[0], jnp.where(place == 1, lists[1], jnp.where(place == 2, misfit, 0.0))
    ).astype(BF16)
    list_copy.start()
    to_side.start()

    blank = jnp.zeros((conv_obs + EXTRA, members), BF16)

    @pl.when(jnp.logical_not(has_north))
    def _():
        for group in range(3):
            conv_buf[group, 0] = blank

    @pl.when(jnp.logical_not(has_south))
    def _():
        for group in range(3):
            conv_buf[group, 2] = blank

    def flip_sat(side):
        sat_flip[:, pl.ds(side * rows, rows)] = sat_buf[side].T

    loads[6].wait()
    flip_sat(0)
    list_copy.wait_recv()
    tile_copy.wait_recv()
    flip_sat(1)

    def relay():
        @pl.when(has_north)
        def _():
            to_south.wait_recv()
            relays[0].start()

        @pl.when(has_south)
        def _():
            to_north.wait_recv()
            relays[1].start()

        @pl.when(outer)
        def _():
            around.wait_recv()

            @pl.when(has_north)
            def _():
                far_north.start()

            @pl.when(has_south)
            def _():
                far_south.start()

    def conv_ready():
        to_side.wait_recv()

        @pl.when(has_north)
        def _():
            relays[0].wait_recv()

        @pl.when(has_south)
        def _():
            relays[1].wait_recv()

        for group in range(2):
            for slot in range(3):
                at = (group * 3 + slot) * conv_obs
                conv_flip[:, at : at + conv_obs] = conv_buf[group, slot, :conv_obs, :].T

    def conv_weight(group, slot, target):
        column = conv_buf[group, slot, conv_obs:, :conv_obs][0:1].astype(F32)
        source = (block, sibling, opposite)[group]
        away = lax.rem(source - target + 1 + n_lon, n_lon) - 1
        row = jnp.floor(column * (1.0 / BLK))
        lat_place = BLK * (slot - 1.0) + row + 0.5 - 0.5 * BLK
        lon_place = BLK * away.astype(F32) + (column - BLK * row) + 0.5 - 0.5 * BLK
        weight = jnp.exp(-(lat_place * lat_place + lon_place * lon_place) / (2.0 * BLK * BLK))
        return jnp.where(away <= 1, weight, 0.0)

    place = iota((EXTRA, LANES), 0)
    eye = iota((half, half), 0) == iota((half, half), 1)
    upper = iota((half, half), 0) <= iota((half, half), 1)

    def add_terms(slot, scaled, spread, forced, first):
        top = dot(scaled[:half], spread)
        low = dot(scaled[half:], spread[:, half:])
        drive = dot(forced, spread)
        diagonal = jnp.sum(jnp.where(eye, low, 0.0), axis=0, keepdims=True)
        pieces = jnp.where(upper, top[:, :half], low), top[:, half:]
        tail = jnp.zeros((EXTRA, LANES), F32)
        for at in range(lane_blocks):
            lanes = slice(at * LANES, (at + 1) * LANES)
            tail += jnp.where(place == at, drive[0:1, lanes], 0.0)
            if at < lane_blocks // 2:
                tail += jnp.where(place == 2 * lane_blocks + at, diagonal[:, lanes], 0.0)
        for at in range(lane_blocks + 1):
            if at < lane_blocks:
                start = (at % (lane_blocks // 2)) * LANES
                term = pieces[at // (lane_blocks // 2)][:, start : start + LANES]
            else:
                term = tail
            into = slice(at * half, at * half + term.shape[0])
            if first:
                acc[slot, into, :] = term
            else:
                acc[slot, into, :] += term

    def add_conv(slot, target, groups):
        weights, pushes = [], []
        for group in groups:
            for side in range(3):
                weight = conv_weight(group, side, target)
                misfit = conv_buf[group, side, conv_obs:, conv_obs : 2 * conv_obs][0:1].astype(F32)
                weights.append(weight)
                pushes.append(weight * misfit)
        spreads = [conv_buf[group, side, :conv_obs, :] for group in groups for side in range(3)]
        flipped = conv_flip[...] if len(groups) == 2 else jnp.concatenate([each.T for each in spreads], axis=1)
        weight = jnp.concatenate(weights, axis=1)
        push = jnp.broadcast_to(jnp.concatenate(pushes, axis=1), (EXTRA, weight.shape[1]))
        scaled = (flipped.astype(F32) * weight).astype(BF16)
        add_terms(slot, scaled, jnp.concatenate(spreads, axis=0), push.astype(BF16), False)

    has_near = jnp.where(core == 0, chip < chips - 1, chip > 0)
    near = chip + 1 - 2 * core

    def compute(slot, to_chip):
        target = 2 * to_chip + core
        name = target.astype(F32)
        weights, pushes = [], []
        for side in range(2):
            lists = sat_lists[side].astype(F32)
            weight = jnp.where(lists[0:1] == name, 1.0, 0.0) + jnp.where(lists[1:2] == name, 0.5, 0.0)
            weights.append(weight)
            pushes.append(weight * lists[2:3])
        weight = jnp.concatenate(weights, axis=1)
        push = jnp.concatenate(pushes, axis=1)
        scaled = sat_flip[...] * weight.astype(BF16)
        spread = sat_buf[...].reshape(2 * rows, members)
        add_terms(slot, scaled, spread, jnp.broadcast_to(push, (EXTRA, 2 * rows)).astype(BF16), True)

        @pl.when(jnp.logical_or(to_chip == chip, to_chip == near))
        def _():
            add_conv(slot, target, (0, 1))

    def line_copy(way, to_chip):
        ahead = block + 2 if way == 0 else block - 2
        return pltpu.make_async_remote_copy(
            src_ref=send_buf.at[way, to_chip], dst_ref=recv_buf.at[way, to_chip],
            send_sem=line_send.at[way, to_chip], recv_sem=line_recv.at[way, to_chip],
            device_id=(band, ahead), device_id_type=MESH,
        )

    def step_of(way, step):
        if way == 0:
            to_chip = chips - 1 + chip - step
            return to_chip, jnp.logical_and(to_chip > chip, to_chip < chips), has_low
        to_chip = step + chip - chips + 1
        return to_chip, jnp.logical_and(to_chip >= 0, to_chip < chip), has_high

    def finish(way, slot, to_chip, behind):
        @pl.when(behind)
        def _():
            line_copy(way, to_chip).wait_recv()
            acc[slot] += recv_buf[way, to_chip].astype(F32)

        tail = acc[slot, lane_blocks * half :, :]
        parts = [tail[at * lane_blocks : (at + 1) * lane_blocks] for at in range(4)]
        high, kept = (parts[at].astype(BF16).astype(F32) for at in (0, 2))
        send_buf[way, to_chip, : lane_blocks * half, :] = acc[slot, : lane_blocks * half, :].astype(BF16)
        send_buf[way, to_chip, lane_blocks * half :, :] = jnp.concatenate(
            [high, parts[0] + parts[1] - high, kept, parts[2] + parts[3] - kept], axis=0
        ).astype(BF16)
        line_copy(way, to_chip).start()

    def step_body(step, carry):
        for way in range(2):
            to_chip, wanted, behind = step_of(way, step)

            @pl.when(wanted)
            def _():
                @pl.when(to_chip == near)
                def _():
                    conv_ready()

                compute(way, to_chip)
        for way in range(2):
            to_chip, wanted, behind = step_of(way, step)

            @pl.when(wanted)
            def _():
                finish(way, way, to_chip, behind)

        if chips > 2:
            @pl.when(step == 0)
            def _():
                relay()

        return carry

    if chips == 2:
        relay()

    lax.fori_loop(0, chips - 1, step_body, 0)

    @pl.when(jnp.logical_not(has_near))
    def _():
        conv_ready()

    compute(0, chip)

    @pl.when(outer)
    def _():
        @pl.when(has_north)
        def _():
            far_south.wait_recv()

        @pl.when(has_south)
        def _():
            far_north.wait_recv()

        add_conv(0, block, (2,))

    @pl.when(has_low)
    def _():
        line_copy(0, chip).wait_recv()
        acc[0] += recv_buf[0, chip].astype(F32)

    @pl.when(has_high)
    def _():
        line_copy(1, chip).wait_recv()
        acc[0] += recv_buf[1, chip].astype(F32)

    out[...] = acc[0]

    tile_copy.wait_send()
    list_copy.wait_send()
    to_side.wait_send()

    @pl.when(outer)
    def _():
        around.wait_send()

        @pl.when(has_north)
        def _():
            far_north.wait_send()

        @pl.when(has_south)
        def _():
            far_south.wait_send()

    @pl.when(has_north)
    def _():
        to_north.wait_send()
        relays[0].wait_send()

    @pl.when(has_south)
    def _():
        to_south.wait_send()
        relays[1].wait_send()

    def drain(step, carry):
        for way in range(2):
            to_chip, wanted, _ = step_of(way, step)

            @pl.when(wanted)
            def _():
                line_copy(way, to_chip).wait_send()
        return carry

    lax.fori_loop(0, chips - 1, drain, 0)


def analyse_kernel(packed, background, out, members_buf, out_buf, load, store):
    members = background.shape[2]
    fetch = pltpu.make_async_copy(background.at[0, 0], members_buf, load)
    fetch.start()
    half, lane_blocks = members // 2, members // LANES
    blocks = [packed[at * half : (at + 1) * half] for at in range(lane_blocks)]
    field = jnp.concatenate(blocks[: lane_blocks // 2], axis=1)
    cross = jnp.concatenate(blocks[lane_blocks // 2 :], axis=1)
    tail = packed[lane_blocks * half :]

    def tail_row(first, count):
        at = [first * lane_blocks + each for each in range(count)]
        return jnp.concatenate(
            [tail[each : each + 1] + tail[each + lane_blocks : each + lane_blocks + 1] for each in at], axis=1
        )

    drive = tail_row(0, lane_blocks)
    diagonal = tail_row(2, lane_blocks // 2)
    row, col = iota((half, half), 0), iota((half, half), 1)
    strict = jnp.where(row < col, field, 0.0)
    under = jnp.where(row > col, field, 0.0)
    first = jnp.where(row <= col, field, 0.0) + strict.T
    second = under + under.T + jnp.where(row == col, diagonal, 0.0)
    gram = jnp.concatenate(
        [jnp.concatenate([first, cross], axis=1), jnp.concatenate([cross.T, second], axis=1)], axis=0
    )
    one = (iota((members, members), 0) == iota((members, members), 1)).astype(F32)
    system = (members - 1.0) * one + gram
    scale = jnp.sqrt(jnp.sum(jnp.sum(system * system, axis=0, keepdims=True), axis=1, keepdims=True))
    y = system / scale
    yb = y.astype(BF16)
    square = dot(yb, yb)
    u = 1.5 * y - 0.5 * square
    w = 0.25 * square - 1.5 * y
    q = 2.25 * u + dot(u.astype(BF16), w.astype(BF16))
    e2 = -0.75 * y - 0.5 * q
    e2b = e2.astype(BF16)
    f = 2.25 * y + dot(yb, e2b)
    h = 4.5 * e2 + dot(e2b, e2b)
    e3 = 1.5 * e2 - 0.5 * (5.0625 * f + dot(f.astype(BF16), h.astype(BF16)))
    e3b = e3.astype(BF16)

    def times_root(vector):
        high = vector.astype(BF16)
        low = (vector - high.astype(F32)).astype(BF16)
        place = iota((16, members), 0)
        both = jnp.where(place == 0, high.astype(F32), jnp.where(place == 1, low.astype(F32), 0.0))
        product = dot(both.astype(BF16), e3b)
        return 3.375 * vector + product[0:1] + product[1:2]

    mean_weight = times_root(times_root(drive)) / scale
    transform = (jnp.sqrt((members - 1.0) / scale) * (3.375 * one + e3)).astype(BF16)

    fetch.wait()
    ensemble = members_buf[...].astype(F32)
    state_mean = jnp.mean(ensemble, axis=0, keepdims=True)
    anomaly = (ensemble - state_mean).astype(BF16)
    high = mean_weight.astype(BF16)
    low = (mean_weight - high.astype(F32)).astype(BF16)
    place = iota((16, members), 0)
    both = jnp.where(place == 0, high.astype(F32), jnp.where(place == 1, low.astype(F32), 0.0))
    shift = dot(both.astype(BF16), anomaly)
    centre = state_mean + shift[0:1] + shift[1:2]
    part = members // STORES
    stores = [
        pltpu.make_async_copy(
            out_buf.at[pl.ds(at * part, part)], out.at[0, 0, pl.ds(at * part, part)], store.at[at]
        )
        for at in range(STORES)
    ]
    for at, copy in enumerate(stores):
        out_buf[at * part : (at + 1) * part, :] = dot(transform[at * part : (at + 1) * part], anomaly) + centre
        copy.start()
    for copy in stores:
        copy.wait()


def shards(
    n_lat, n_lon,
    background, conv_pert, conv_misfit, conv_column, sat_pert, sat_misfit, sat_rows, sat_targets,
):
    members, cells = background.shape[2:]
    tiles, tile_obs = sat_pert.shape[1:3]
    conv_obs = conv_pert.shape[2]
    rows, chips, half = tiles * tile_obs, n_lon // 2, members // 2
    vmem = pl.BlockSpec(memory_space=pltpu.VMEM)
    lanes_long = members // LANES * half + EXTRA
    hbm = pl.BlockSpec(memory_space=pltpu.HBM)
    packed = pl.pallas_call(
        functools.partial(gather_kernel, n_lat, n_lon),
        out_shape=jax.ShapeDtypeStruct((lanes_long, LANES), F32),
        in_specs=[hbm] * 7,
        out_specs=vmem,
        scratch_shapes=[
            pltpu.VMEM((1, 1, conv_obs), BF16),
            pltpu.VMEM((1, 1, conv_obs), jnp.int32),
            pltpu.VMEM((1, tiles, tile_obs), BF16),
            pltpu.VMEM((1, tiles), jnp.int32),
            pltpu.VMEM((1, 2, tiles), jnp.int32),
            pltpu.VMEM((2, rows, members), BF16),
            pltpu.VMEM((2, EXTRA, rows), BF16),
            pltpu.VMEM((3, 3, conv_obs + EXTRA, members), BF16),
            pltpu.VMEM((members, 2 * rows), BF16),
            pltpu.VMEM((members, 6 * conv_obs), BF16),
            pltpu.VMEM((2, lanes_long, LANES), F32),
            pltpu.VMEM((2, chips, lanes_long, LANES), BF16),
            pltpu.VMEM((2, chips, lanes_long, LANES), BF16),
            pltpu.SemaphoreType.DMA((7,)),
            pltpu.SemaphoreType.DMA((2,)),
            pltpu.SemaphoreType.DMA((2,)),
            pltpu.SemaphoreType.DMA((8,)),
            pltpu.SemaphoreType.DMA((8,)),
            pltpu.SemaphoreType.DMA((2, chips)),
            pltpu.SemaphoreType.DMA((2, chips)),
        ],
        compiler_params=pltpu.CompilerParams(
            collective_id=0, has_side_effects=True, vmem_limit_bytes=64 * 1024 * 1024
        ),
        cost_estimate=pl.CostEstimate(
            flops=2 * (chips * 2 * rows + 9 * conv_obs) * members * members,
            bytes_accessed=4 * rows * members, transcendentals=0,
        ),
        name="gather_grams",
    )(
        conv_pert, conv_misfit, conv_column, sat_pert.reshape(rows, members), sat_misfit, sat_rows,
        jnp.swapaxes(sat_targets, 1, 2),
    )
    return pl.pallas_call(
        analyse_kernel,
        out_shape=jax.ShapeDtypeStruct((1, 1, members, cells), F32),
        in_specs=[vmem, hbm],
        out_specs=hbm,
        scratch_shapes=[
            pltpu.VMEM((members, cells), BF16),
            pltpu.VMEM((members, cells), F32),
            pltpu.SemaphoreType.DMA,
            pltpu.SemaphoreType.DMA((STORES,)),
        ],
        compiler_params=pltpu.CompilerParams(vmem_limit_bytes=64 * 1024 * 1024),
        cost_estimate=pl.CostEstimate(
            flops=14 * members * members * members, bytes_accessed=6 * members * cells, transcendentals=0
        ),
        name="analyse",
    )(packed, background)


def solution(mesh):
    placed = (
        P("lat", "lon", None, None),
        P("lat", "lon", None, None),
        P("lat", "lon", None),
        P("lat", "lon", None),
        P("lat", "lon", None, None),
        P("lat", "lon", None),
        P("lat", "lon"),
        P("lat", "lon", None),
    )
    return jax.shard_map(
        functools.partial(shards, mesh.shape["lat"], mesh.shape["lon"]),
        mesh=mesh, in_specs=placed, out_specs=P("lat", "lon", None, None), check_vma=False,
    )
```

```python
import functools

import jax
import jax.numpy as jnp
from jax import lax
from jax.experimental import pallas as pl
from jax.experimental.pallas import tpu as pltpu
from jax.sharding import PartitionSpec as P

BLK = 16
MESH = pl.DeviceIdType.MESH
F32 = jnp.float32
BF16 = jnp.bfloat16
EXTRA = 16
LANES = 128
STORES = 4


def dot(left, right):
    return lax.dot_general(left, right, (((1,), (0,)), ((), ())), preferred_element_type=F32)


def iota(shape, dim):
    return lax.broadcasted_iota(jnp.int32, shape, dim)


def gather_kernel(
    n_lat, n_lon,
    background, conv_pert, conv_misfit, conv_column, sat_pert, sat_misfit, sat_rows, sat_targets,
    out, anomaly, centre,
    members_buf, anomaly_buf, small_misfit, small_column, tile_misfit, tile_rows, tile_targets,
    sat_buf, sat_lists, conv_buf, sat_flip, conv_flip, acc, send_buf, recv_buf,
    load, sat_send, sat_recv, conv_send, conv_recv, line_send, line_recv,
):
    chips = n_lon // 2
    band = lax.axis_index("lat")
    block = lax.axis_index("lon")
    chip, core = block // 2, block % 2
    sibling = 2 * chip + (1 - core)
    opposite = n_lon - 1 - block
    tiles, tile_obs = sat_misfit.shape[1], sat_misfit.shape[2]
    rows, members = tiles * tile_obs, sat_pert.shape[1]
    conv_obs = conv_pert.shape[2]
    half, lane_blocks = members // 2, members // LANES
    has_north, has_south = band > 0, band < n_lat - 1
    has_low, has_high = chip > 0, chip < chips - 1
    outer = jnp.logical_or(block == 0, block == n_lon - 1)
    mates = (
        (has_north, (band - 1, block)),
        (has_south, (band + 1, block)),
        (has_low, (band, block - 2)),
        (has_high, (band, block + 2)),
        (outer, (band, opposite)),
    )

    barrier = pltpu.get_barrier_semaphore()
    pl.semaphore_signal(barrier, inc=1, device_id=(band, sibling), device_id_type=MESH)
    for here, mate in mates:
        @pl.when(here)
        def _():
            pl.semaphore_signal(barrier, inc=1, device_id=mate, device_id_type=MESH)

    loads = [
        pltpu.make_async_copy(source, target, load.at[at])
        for at, (source, target) in enumerate(
            (
                (conv_pert.at[0, 0], conv_buf.at[0, 1, pl.ds(0, conv_obs)]),
                (conv_misfit, small_misfit),
                (conv_column, small_column),
                (sat_misfit, tile_misfit),
                (sat_rows, tile_rows),
                (sat_targets, tile_targets),
                (sat_pert, sat_buf.at[0]),
                (background.at[0, 0], members_buf),
            )
        )
    ]
    for copy in loads:
        copy.start()
    pl.semaphore_wait(barrier, 1 + sum(here.astype(jnp.int32) for here, _ in mates))

    def sat_copy(source, target, at):
        return pltpu.make_async_remote_copy(
            src_ref=source, dst_ref=target, send_sem=sat_send.at[at], recv_sem=sat_recv.at[at],
            device_id=(band, sibling), device_id_type=MESH,
        )

    tile_copy = sat_copy(sat_pert, sat_buf.at[1], 0)
    list_copy = sat_copy(sat_lists.at[0], sat_lists.at[1], 1)
    tile_copy.start()

    for copy in loads[:6]:
        copy.wait()
    conv_buf[0, 1, conv_obs:, :] = jnp.concatenate(
        [
            jnp.broadcast_to(small_column[0].astype(F32).astype(BF16), (EXTRA, conv_obs)),
            jnp.broadcast_to(small_misfit[0], (EXTRA, conv_obs)),
            jnp.zeros((EXTRA, members - 2 * conv_obs), BF16),
        ],
        axis=1,
    )

    def conv_copy(group, slot, to_group, to_slot, sem, mate):
        return pltpu.make_async_remote_copy(
            src_ref=conv_buf.at[group, slot], dst_ref=conv_buf.at[to_group, to_slot],
            send_sem=conv_send.at[sem], recv_sem=conv_recv.at[sem],
            device_id=mate, device_id_type=MESH,
        )

    to_north = conv_copy(0, 1, 0, 2, 0, (band - 1, block))
    to_south = conv_copy(0, 1, 0, 0, 1, (band + 1, block))
    to_side = conv_copy(0, 1, 1, 1, 2, (band, sibling))
    relays = [conv_copy(0, 0, 1, 0, 3, (band, sibling)), conv_copy(0, 2, 1, 2, 4, (band, sibling))]
    around = conv_copy(0, 1, 2, 1, 5, (band, opposite))
    far_north = conv_copy(2, 1, 2, 2, 6, (band - 1, block))
    far_south = conv_copy(2, 1, 2, 0, 7, (band + 1, block))

    @pl.when(outer)
    def _():
        around.start()

    @pl.when(has_north)
    def _():
        to_north.start()

    @pl.when(has_south)
    def _():
        to_south.start()

    own_tile = iota((tiles, rows), 1) // tile_obs == iota((tiles, rows), 0)
    own_mask = own_tile.astype(BF16)
    spread_obs = (iota((tile_obs, rows), 1) % tile_obs == iota((tile_obs, rows), 0)).astype(BF16)
    misfit = jnp.sum(jnp.where(own_tile, dot(tile_misfit[0], spread_obs), 0.0), axis=0, keepdims=True)
    count = dot(jnp.broadcast_to(tile_rows[...].astype(F32).astype(BF16), (8, tiles)), own_mask)[0:1]
    live = (iota((1, rows), 1) % tile_obs).astype(F32) < count
    names = tile_targets[0].astype(F32)
    lists = [
        jnp.where(
            live,
            dot(jnp.broadcast_to(names[e : e + 1], (8, tiles)).astype(BF16), own_mask)[0:1],
            -1.0,
        )
        for e in range(2)
    ]
    place = iota((EXTRA, rows), 0)
    sat_lists[0] = jnp.where(
        place == 0, lists[0], jnp.where(place == 1, lists[1], jnp.where(place == 2, misfit, 0.0))
    ).astype(BF16)
    list_copy.start()
    to_side.start()

    blank = jnp.zeros((conv_obs + EXTRA, members), BF16)

    @pl.when(jnp.logical_not(has_north))
    def _():
        for group in range(3):
            conv_buf[group, 0] = blank

    @pl.when(jnp.logical_not(has_south))
    def _():
        for group in range(3):
            conv_buf[group, 2] = blank

    def flip_sat(side):
        sat_flip[side] = sat_buf[side].T

    def relay():
        @pl.when(has_north)
        def _():
            to_south.wait_recv()
            relays[0].start()

        @pl.when(has_south)
        def _():
            to_north.wait_recv()
            relays[1].start()

        @pl.when(outer)
        def _():
            around.wait_recv()

            @pl.when(has_north)
            def _():
                far_north.start()

            @pl.when(has_south)
            def _():
                far_south.start()

    def conv_ready():
        to_side.wait_recv()

        @pl.when(has_north)
        def _():
            relays[0].wait_recv()

        @pl.when(has_south)
        def _():
            relays[1].wait_recv()

        for group in range(2):
            for slot in range(3):
                at = (group * 3 + slot) * conv_obs
                conv_flip[:, at : at + conv_obs] = conv_buf[group, slot, :conv_obs, :].T

    def conv_weight(group, slot, target):
        column = conv_buf[group, slot, conv_obs:, :conv_obs][0:1].astype(F32)
        source = (block, sibling, opposite)[group]
        away = lax.rem(source - target + 1 + n_lon, n_lon) - 1
        row = jnp.floor(column * (1.0 / BLK))
        lat_place = BLK * (slot - 1.0) + row + 0.5 - 0.5 * BLK
        lon_place = BLK * away.astype(F32) + (column - BLK * row) + 0.5 - 0.5 * BLK
        weight = jnp.exp(-(lat_place * lat_place + lon_place * lon_place) / (2.0 * BLK * BLK))
        return jnp.where(away <= 1, weight, 0.0)

    place = iota((EXTRA, LANES), 0)
    eye = iota((half, half), 0) == iota((half, half), 1)
    upper = iota((half, half), 0) <= iota((half, half), 1)

    cut = lane_blocks // 2 * half
    parts = (slice(0, cut), slice(cut, 2 * cut + EXTRA))

    def add_terms(slot, part, flipped, weight, push, spread, first):
        def put(into, term):
            if first:
                acc[slot, into, :] = term
            else:
                acc[slot, into, :] += term

        def scaled(rows_of):
            if weight.dtype == BF16:
                return rows_of * weight
            return (rows_of.astype(F32) * weight).astype(BF16)

        if part == 0:
            piece = dot(scaled(flipped[:half]), spread[:, half:])
        else:
            low = dot(scaled(flipped[half:]), spread[:, half:])
            piece = jnp.where(upper, dot(scaled(flipped[:half]), spread[:, :half]), low)
            drive = dot(jnp.broadcast_to(push, (EXTRA, push.shape[1])).astype(BF16), spread)
            diagonal = jnp.sum(jnp.where(eye, low, 0.0), axis=0, keepdims=True)
            tail = jnp.zeros((EXTRA, LANES), F32)
            for at in range(lane_blocks):
                lanes = slice(at * LANES, (at + 1) * LANES)
                tail += jnp.where(place == at, drive[0:1, lanes], 0.0)
                if at < lane_blocks // 2:
                    tail += jnp.where(place == 2 * lane_blocks + at, diagonal[:, lanes], 0.0)
            put(slice(2 * cut, 2 * cut + EXTRA), tail)
        for at in range(lane_blocks // 2):
            put(slice(part * cut + at * half, part * cut + (at + 1) * half), piece[:, at * LANES : (at + 1) * LANES])

    def add_conv(slot, part, target, groups):
        weights, pushes = [], []
        for group in groups:
            for side in range(3):
                weight = conv_weight(group, side, target)
                misfit = conv_buf[group, side, conv_obs:, conv_obs : 2 * conv_obs][0:1].astype(F32)
                weights.append(weight)
                pushes.append(weight * misfit)
        spreads = [conv_buf[group, side, :conv_obs, :] for group in groups for side in range(3)]
        flipped = conv_flip[...] if len(groups) == 2 else jnp.concatenate([each.T for each in spreads], axis=1)
        weight, push = (jnp.concatenate(each, axis=1) for each in (weights, pushes))
        add_terms(slot, part, flipped, weight, push, jnp.concatenate(spreads, axis=0), False)

    def add_sat(slot, part, to_chip, side):
        name = (2 * to_chip + core).astype(F32)
        lists = sat_lists[side].astype(F32)
        weight = jnp.where(lists[0:1] == name, 1.0, 0.0) + jnp.where(lists[1:2] == name, 0.5, 0.0)
        add_terms(
            slot, part, sat_flip[side], weight.astype(BF16), weight * lists[2:3], sat_buf[side], side == 0
        )

    has_near = jnp.where(core == 0, chip < chips - 1, chip > 0)
    near = chip + 1 - 2 * core

    def line_copy(way, to_chip, part):
        ahead = block + 2 if way == 0 else block - 2
        span = pl.ds(parts[part].start, parts[part].stop - parts[part].start)
        return pltpu.make_async_remote_copy(
            src_ref=send_buf.at[way, to_chip, span], dst_ref=recv_buf.at[way, to_chip, span],
            send_sem=line_send.at[way, to_chip, part], recv_sem=line_recv.at[way, to_chip, part],
            device_id=(band, ahead), device_id_type=MESH,
        )

    def step_of(way, step):
        if way == 0:
            to_chip = chips - 1 + chip - step
            return to_chip, jnp.logical_and(to_chip > chip, to_chip < chips), has_low
        to_chip = step + chip - chips + 1
        return to_chip, jnp.logical_and(to_chip >= 0, to_chip < chip), has_high

    def finish(way, to_chip, behind, part):
        @pl.when(behind)
        def _():
            line_copy(way, to_chip, part).wait_recv()
            acc[way, parts[part], :] += recv_buf[way, to_chip, parts[part], :].astype(F32)

        send_buf[way, to_chip, part * cut : (part + 1) * cut, :] = acc[
            way, part * cut : (part + 1) * cut, :
        ].astype(BF16)
        if part == 1:
            tail = acc[way, 2 * cut :, :]
            four = [tail[at * lane_blocks : (at + 1) * lane_blocks] for at in range(4)]
            high, kept = (four[at].astype(BF16).astype(F32) for at in (0, 2))
            send_buf[way, to_chip, 2 * cut :, :] = jnp.concatenate(
                [high, four[0] + four[1] - high, kept, four[2] + four[3] - kept], axis=0
            ).astype(BF16)
        line_copy(way, to_chip, part).start()

    loads[6].wait()
    flip_sat(0)
    for way in range(2):
        to_chip, wanted, _ = step_of(way, 0)

        @pl.when(wanted)
        def _():
            for part in range(2):
                add_sat(way, part, to_chip, 0)

    list_copy.wait_recv()
    tile_copy.wait_recv()
    flip_sat(1)

    def step_body(step, carry):
        for part in range(2):
            for way in range(2):
                to_chip, wanted, behind = step_of(way, step)

                @pl.when(wanted)
                def _():
                    @pl.when(step > 0)
                    def _():
                        add_sat(way, part, to_chip, 0)

                    add_sat(way, part, to_chip, 1)

                    @pl.when(to_chip == near)
                    def _():
                        if part == 0:
                            conv_ready()
                        add_conv(way, part, 2 * to_chip + core, (0, 1))

            for way in range(2):
                to_chip, wanted, behind = step_of(way, step)

                @pl.when(wanted)
                def _():
                    finish(way, to_chip, behind, part)

        if chips > 2:
            @pl.when(step == 0)
            def _():
                relay()

        return carry

    if chips == 2:
        relay()

    lax.fori_loop(0, chips - 1, step_body, 0)

    @pl.when(jnp.logical_not(has_near))
    def _():
        conv_ready()

    for part in range(2):
        for side in range(2):
            add_sat(0, part, chip, side)
        add_conv(0, part, block, (0, 1))

    @pl.when(outer)
    def _():
        @pl.when(has_north)
        def _():
            far_south.wait_recv()

        @pl.when(has_south)
        def _():
            far_north.wait_recv()

        for part in range(2):
            add_conv(0, part, block, (2,))

    loads[7].wait()
    ensemble = members_buf[...].astype(F32)
    state_mean = jnp.mean(ensemble, axis=0, keepdims=True)
    anomaly_buf[...] = (ensemble - state_mean).astype(BF16)
    keep = pltpu.make_async_copy(anomaly_buf, anomaly, load.at[8])
    keep.start()
    centre[...] = jnp.broadcast_to(state_mean, centre.shape)

    for part in range(2):
        for way, behind in enumerate((has_low, has_high)):
            @pl.when(behind)
            def _():
                line_copy(way, chip, part).wait_recv()
                acc[0, parts[part], :] += recv_buf[way, chip, parts[part], :].astype(F32)

        out[parts[part], :] = acc[0, parts[part], :]

    keep.wait()
    tile_copy.wait_send()
    list_copy.wait_send()
    to_side.wait_send()

    @pl.when(outer)
    def _():
        around.wait_send()

        @pl.when(has_north)
        def _():
            far_north.wait_send()

        @pl.when(has_south)
        def _():
            far_south.wait_send()

    @pl.when(has_north)
    def _():
        to_north.wait_send()
        relays[0].wait_send()

    @pl.when(has_south)
    def _():
        to_south.wait_send()
        relays[1].wait_send()

    def drain(step, carry):
        for way in range(2):
            to_chip, wanted, _ = step_of(way, step)

            @pl.when(wanted)
            def _():
                for part in range(2):
                    line_copy(way, to_chip, part).wait_send()
        return carry

    lax.fori_loop(0, chips - 1, drain, 0)


def analyse_kernel(packed, state_mean, spread, out, anomaly_buf, out_buf, load, store):
    members = spread.shape[0]
    fetch = pltpu.make_async_copy(spread, anomaly_buf, load)
    fetch.start()
    half, lane_blocks = members // 2, members // LANES
    blocks = [packed[at * half : (at + 1) * half] for at in range(lane_blocks)]
    cross = jnp.concatenate(blocks[: lane_blocks // 2], axis=1)
    field = jnp.concatenate(blocks[lane_blocks // 2 :], axis=1)
    tail = packed[lane_blocks * half :]

    def tail_row(first, count):
        at = [first * lane_blocks + each for each in range(count)]
        return jnp.concatenate(
            [tail[each : each + 1] + tail[each + lane_blocks : each + lane_blocks + 1] for each in at], axis=1
        )

    drive = tail_row(0, lane_blocks)
    diagonal = tail_row(2, lane_blocks // 2)
    row, col = iota((half, half), 0), iota((half, half), 1)
    strict = jnp.where(row < col, field, 0.0)
    under = jnp.where(row > col, field, 0.0)
    first = jnp.where(row <= col, field, 0.0) + strict.T
    second = under + under.T + jnp.where(row == col, diagonal, 0.0)
    gram = jnp.concatenate(
        [jnp.concatenate([first, cross], axis=1), jnp.concatenate([cross.T, second], axis=1)], axis=0
    )
    one = (iota((members, members), 0) == iota((members, members), 1)).astype(F32)
    system = (members - 1.0) * one + gram
    scale = jnp.sqrt(jnp.sum(jnp.sum(system * system, axis=0, keepdims=True), axis=1, keepdims=True))
    y = system / scale
    yb = y.astype(BF16)
    square = dot(yb, yb)
    u = 1.5 * y - 0.5 * square
    w = 0.25 * square - 1.5 * y
    q = 2.25 * u + dot(u.astype(BF16), w.astype(BF16))
    e2 = -0.75 * y - 0.5 * q
    e2b = e2.astype(BF16)
    f = 2.25 * y + dot(yb, e2b)
    h = 4.5 * e2 + dot(e2b, e2b)
    e3 = 1.5 * e2 - 0.5 * (5.0625 * f + dot(f.astype(BF16), h.astype(BF16)))
    e3b = e3.astype(BF16)

    def times_root(vector):
        high = vector.astype(BF16)
        low = (vector - high.astype(F32)).astype(BF16)
        place = iota((16, members), 0)
        both = jnp.where(place == 0, high.astype(F32), jnp.where(place == 1, low.astype(F32), 0.0))
        product = dot(both.astype(BF16), e3b)
        return 3.375 * vector + product[0:1] + product[1:2]

    mean_weight = times_root(times_root(drive)) / scale
    transform = (jnp.sqrt((members - 1.0) / scale) * (3.375 * one + e3)).astype(BF16)

    fetch.wait()
    anomaly = anomaly_buf[...]
    high = mean_weight.astype(BF16)
    low = (mean_weight - high.astype(F32)).astype(BF16)
    place = iota((16, members), 0)
    both = jnp.where(place == 0, high.astype(F32), jnp.where(place == 1, low.astype(F32), 0.0))
    shift = dot(both.astype(BF16), anomaly)
    centre = state_mean[0:1] + shift[0:1] + shift[1:2]
    part = members // STORES
    stores = [
        pltpu.make_async_copy(
            out_buf.at[pl.ds(at * part, part)], out.at[0, 0, pl.ds(at * part, part)], store.at[at]
        )
        for at in range(STORES)
    ]
    for at, copy in enumerate(stores):
        out_buf[at * part : (at + 1) * part, :] = dot(transform[at * part : (at + 1) * part], anomaly) + centre
        copy.start()
    for copy in stores:
        copy.wait()


def shards(
    n_lat, n_lon,
    background, conv_pert, conv_misfit, conv_column, sat_pert, sat_misfit, sat_rows, sat_targets,
):
    members, cells = background.shape[2:]
    tiles, tile_obs = sat_pert.shape[1:3]
    conv_obs = conv_pert.shape[2]
    rows, chips, half = tiles * tile_obs, n_lon // 2, members // 2
    vmem = pl.BlockSpec(memory_space=pltpu.VMEM)
    lanes_long = members // LANES * half + EXTRA
    hbm = pl.BlockSpec(memory_space=pltpu.HBM)
    packed, anomaly, state_mean = pl.pallas_call(
        functools.partial(gather_kernel, n_lat, n_lon),
        out_shape=(
            jax.ShapeDtypeStruct((lanes_long, LANES), F32),
            jax.ShapeDtypeStruct((members, cells), BF16),
            jax.ShapeDtypeStruct((8, cells), F32),
        ),
        in_specs=[hbm] * 8,
        out_specs=(vmem, hbm, vmem),
        scratch_shapes=[
            pltpu.VMEM((members, cells), BF16),
            pltpu.VMEM((members, cells), BF16),
            pltpu.VMEM((1, 1, conv_obs), BF16),
            pltpu.VMEM((1, 1, conv_obs), jnp.int32),
            pltpu.VMEM((1, tiles, tile_obs), BF16),
            pltpu.VMEM((1, tiles), jnp.int32),
            pltpu.VMEM((1, 2, tiles), jnp.int32),
            pltpu.VMEM((2, rows, members), BF16),
            pltpu.VMEM((2, EXTRA, rows), BF16),
            pltpu.VMEM((3, 3, conv_obs + EXTRA, members), BF16),
            pltpu.VMEM((2, members, rows), BF16),
            pltpu.VMEM((members, 6 * conv_obs), BF16),
            pltpu.VMEM((2, lanes_long, LANES), F32),
            pltpu.VMEM((2, chips, lanes_long, LANES), BF16),
            pltpu.VMEM((2, chips, lanes_long, LANES), BF16),
            pltpu.SemaphoreType.DMA((9,)),
            pltpu.SemaphoreType.DMA((2,)),
            pltpu.SemaphoreType.DMA((2,)),
            pltpu.SemaphoreType.DMA((8,)),
            pltpu.SemaphoreType.DMA((8,)),
            pltpu.SemaphoreType.DMA((2, chips, 2)),
            pltpu.SemaphoreType.DMA((2, chips, 2)),
        ],
        compiler_params=pltpu.CompilerParams(
            collective_id=0, has_side_effects=True, vmem_limit_bytes=64 * 1024 * 1024
        ),
        cost_estimate=pl.CostEstimate(
            flops=2 * (chips * 2 * rows + 9 * conv_obs) * members * members,
            bytes_accessed=4 * rows * members, transcendentals=0,
        ),
        name="gather_grams",
    )(
        background, conv_pert, conv_misfit, conv_column, sat_pert.reshape(rows, members), sat_misfit, sat_rows,
        jnp.swapaxes(sat_targets, 1, 2),
    )
    return pl.pallas_call(
        analyse_kernel,
        out_shape=jax.ShapeDtypeStruct((1, 1, members, cells), F32),
        in_specs=[vmem, vmem, hbm],
        out_specs=hbm,
        scratch_shapes=[
            pltpu.VMEM((members, cells), BF16),
            pltpu.VMEM((members, cells), F32),
            pltpu.SemaphoreType.DMA,
            pltpu.SemaphoreType.DMA((STORES,)),
        ],
        compiler_params=pltpu.CompilerParams(vmem_limit_bytes=64 * 1024 * 1024),
        cost_estimate=pl.CostEstimate(
            flops=14 * members * members * members, bytes_accessed=6 * members * cells, transcendentals=0
        ),
        name="analyse",
    )(packed, state_mean, anomaly)


def solution(mesh):
    placed = (
        P("lat", "lon", None, None),
        P("lat", "lon", None, None),
        P("lat", "lon", None),
        P("lat", "lon", None),
        P("lat", "lon", None, None),
        P("lat", "lon", None),
        P("lat", "lon"),
        P("lat", "lon", None),
    )
    return jax.shard_map(
        functools.partial(shards, mesh.shape["lat"], mesh.shape["lon"]),
        mesh=mesh, in_specs=placed, out_specs=P("lat", "lon", None, None), check_vma=False,
    )
```

```python
import functools

import jax
import jax.numpy as jnp
from jax import lax
from jax.experimental import pallas as pl
from jax.experimental.pallas import tpu as pltpu
from jax.sharding import PartitionSpec as P

BLK = 16
MESH = pl.DeviceIdType.MESH
F32 = jnp.float32
BF16 = jnp.bfloat16
EXTRA = 16
LANES = 128
STORES = 4


def dot(left, right):
    return lax.dot_general(left, right, (((1,), (0,)), ((), ())), preferred_element_type=F32)


def iota(shape, dim):
    return lax.broadcasted_iota(jnp.int32, shape, dim)


def gather_kernel(
    n_lat, n_lon,
    background, conv_pert, conv_misfit, conv_column, sat_pert, sat_misfit, sat_rows, sat_targets,
    out, anomaly, centre,
    members_buf, anomaly_buf, small_misfit, small_column, tile_misfit, tile_rows, tile_targets,
    sat_buf, sat_lists, conv_buf, sat_flip, conv_flip, acc, send_buf, recv_buf,
    load, sat_send, sat_recv, conv_send, conv_recv, line_send, line_recv,
):
    chips = n_lon // 2
    band = lax.axis_index("lat")
    block = lax.axis_index("lon")
    chip, core = block // 2, block % 2
    sibling = 2 * chip + (1 - core)
    opposite = n_lon - 1 - block
    tiles, tile_obs = sat_misfit.shape[1], sat_misfit.shape[2]
    rows, members = tiles * tile_obs, sat_pert.shape[1]
    conv_obs = conv_pert.shape[2]
    half, lane_blocks = members // 2, members // LANES
    has_north, has_south = band > 0, band < n_lat - 1
    has_low, has_high = chip > 0, chip < chips - 1
    outer = jnp.logical_or(block == 0, block == n_lon - 1)
    mates = (
        (has_north, (band - 1, block)),
        (has_south, (band + 1, block)),
        (has_low, (band, block - 2)),
        (has_high, (band, block + 2)),
        (outer, (band, opposite)),
    )

    barrier = pltpu.get_barrier_semaphore()
    pl.semaphore_signal(barrier, inc=1, device_id=(band, sibling), device_id_type=MESH)
    for here, mate in mates:
        @pl.when(here)
        def _():
            pl.semaphore_signal(barrier, inc=1, device_id=mate, device_id_type=MESH)

    loads = [
        pltpu.make_async_copy(source, target, load.at[at])
        for at, (source, target) in enumerate(
            (
                (conv_pert.at[0, 0], conv_buf.at[0, 1, pl.ds(0, conv_obs)]),
                (conv_misfit, small_misfit),
                (conv_column, small_column),
                (sat_misfit, tile_misfit),
                (sat_rows, tile_rows),
                (sat_targets, tile_targets),
                (sat_pert, sat_buf.at[0]),
                (background.at[0, 0], members_buf),
            )
        )
    ]
    for copy in loads:
        copy.start()
    pl.semaphore_wait(barrier, 1 + sum(here.astype(jnp.int32) for here, _ in mates))

    def sat_copy(source, target, at):
        return pltpu.make_async_remote_copy(
            src_ref=source, dst_ref=target, send_sem=sat_send.at[at], recv_sem=sat_recv.at[at],
            device_id=(band, sibling), device_id_type=MESH,
        )

    tile_copy = sat_copy(sat_pert, sat_buf.at[1], 0)
    list_copy = sat_copy(sat_lists.at[0], sat_lists.at[1], 1)
    tile_copy.start()

    for copy in loads[:6]:
        copy.wait()
    conv_buf[0, 1, conv_obs:, :] = jnp.concatenate(
        [
            jnp.broadcast_to(small_column[0].astype(F32).astype(BF16), (EXTRA, conv_obs)),
            jnp.broadcast_to(small_misfit[0], (EXTRA, conv_obs)),
            jnp.zeros((EXTRA, members - 2 * conv_obs), BF16),
        ],
        axis=1,
    )

    def conv_copy(group, slot, to_group, to_slot, sem, mate):
        return pltpu.make_async_remote_copy(
            src_ref=conv_buf.at[group, slot], dst_ref=conv_buf.at[to_group, to_slot],
            send_sem=conv_send.at[sem], recv_sem=conv_recv.at[sem],
            device_id=mate, device_id_type=MESH,
        )

    to_north = conv_copy(0, 1, 0, 2, 0, (band - 1, block))
    to_south = conv_copy(0, 1, 0, 0, 1, (band + 1, block))
    to_side = conv_copy(0, 1, 1, 1, 2, (band, sibling))
    relays = [conv_copy(0, 0, 1, 0, 3, (band, sibling)), conv_copy(0, 2, 1, 2, 4, (band, sibling))]
    around = conv_copy(0, 1, 2, 1, 5, (band, opposite))
    far_north = conv_copy(2, 1, 2, 2, 6, (band - 1, block))
    far_south = conv_copy(2, 1, 2, 0, 7, (band + 1, block))

    @pl.when(outer)
    def _():
        around.start()

    @pl.when(has_north)
    def _():
        to_north.start()

    @pl.when(has_south)
    def _():
        to_south.start()

    own_tile = iota((tiles, rows), 1) // tile_obs == iota((tiles, rows), 0)
    own_mask = own_tile.astype(BF16)
    spread_obs = (iota((tile_obs, rows), 1) % tile_obs == iota((tile_obs, rows), 0)).astype(BF16)
    misfit = jnp.sum(jnp.where(own_tile, dot(tile_misfit[0], spread_obs), 0.0), axis=0, keepdims=True)
    count = dot(jnp.broadcast_to(tile_rows[...].astype(F32).astype(BF16), (8, tiles)), own_mask)[0:1]
    live = (iota((1, rows), 1) % tile_obs).astype(F32) < count
    names = tile_targets[0].astype(F32)
    lists = [
        jnp.where(
            live,
            dot(jnp.broadcast_to(names[e : e + 1], (8, tiles)).astype(BF16), own_mask)[0:1],
            -1.0,
        )
        for e in range(2)
    ]
    place = iota((EXTRA, rows), 0)
    sat_lists[0] = jnp.where(
        place == 0, lists[0], jnp.where(place == 1, lists[1], jnp.where(place == 2, misfit, 0.0))
    ).astype(BF16)
    list_copy.start()
    to_side.start()

    blank = jnp.zeros((conv_obs + EXTRA, members), BF16)

    @pl.when(jnp.logical_not(has_north))
    def _():
        for group in range(3):
            conv_buf[group, 0] = blank

    @pl.when(jnp.logical_not(has_south))
    def _():
        for group in range(3):
            conv_buf[group, 2] = blank

    def flip_sat(side):
        sat_flip[side] = sat_buf[side].T

    def relay():
        @pl.when(has_north)
        def _():
            to_south.wait_recv()
            relays[0].start()

        @pl.when(has_south)
        def _():
            to_north.wait_recv()
            relays[1].start()

        @pl.when(outer)
        def _():
            around.wait_recv()

            @pl.when(has_north)
            def _():
                far_north.start()

            @pl.when(has_south)
            def _():
                far_south.start()

    def conv_ready():
        to_side.wait_recv()

        @pl.when(has_north)
        def _():
            relays[0].wait_recv()

        @pl.when(has_south)
        def _():
            relays[1].wait_recv()

        for group in range(2):
            for slot in range(3):
                at = (group * 3 + slot) * conv_obs
                conv_flip[:, at : at + conv_obs] = conv_buf[group, slot, :conv_obs, :].T

    def conv_weight(group, slot, target):
        column = conv_buf[group, slot, conv_obs:, :conv_obs][0:1].astype(F32)
        source = (block, sibling, opposite)[group]
        away = lax.rem(source - target + 1 + n_lon, n_lon) - 1
        row = jnp.floor(column * (1.0 / BLK))
        lat_place = BLK * (slot - 1.0) + row + 0.5 - 0.5 * BLK
        lon_place = BLK * away.astype(F32) + (column - BLK * row) + 0.5 - 0.5 * BLK
        weight = jnp.exp(-(lat_place * lat_place + lon_place * lon_place) / (2.0 * BLK * BLK))
        return jnp.where(away <= 1, weight, 0.0)

    place = iota((EXTRA, LANES), 0)
    eye = iota((half, half), 0) == iota((half, half), 1)
    upper = iota((half, half), 0) <= iota((half, half), 1)

    cut = lane_blocks // 2 * half
    parts = (slice(0, cut), slice(cut, 2 * cut + EXTRA))

    def add_terms(slot, part, flipped, weight, push, spread, first):
        def put(into, term):
            if first:
                acc[slot, into, :] = term
            else:
                acc[slot, into, :] += term

        def scaled(rows_of):
            if weight.dtype == BF16:
                return rows_of * weight
            return (rows_of.astype(F32) * weight).astype(BF16)

        if part == 0:
            piece = dot(scaled(flipped[:half]), spread[:, half:])
        else:
            low = dot(scaled(flipped[half:]), spread[:, half:])
            piece = jnp.where(upper, dot(scaled(flipped[:half]), spread[:, :half]), low)
            drive = dot(jnp.broadcast_to(push, (EXTRA, push.shape[1])).astype(BF16), spread)
            diagonal = jnp.sum(jnp.where(eye, low, 0.0), axis=0, keepdims=True)
            tail = jnp.zeros((EXTRA, LANES), F32)
            for at in range(lane_blocks):
                lanes = slice(at * LANES, (at + 1) * LANES)
                tail += jnp.where(place == at, drive[0:1, lanes], 0.0)
                if at < lane_blocks // 2:
                    tail += jnp.where(place == 2 * lane_blocks + at, diagonal[:, lanes], 0.0)
            put(slice(2 * cut, 2 * cut + EXTRA), tail)
        for at in range(lane_blocks // 2):
            put(slice(part * cut + at * half, part * cut + (at + 1) * half), piece[:, at * LANES : (at + 1) * LANES])

    def add_conv(slot, part, target, groups):
        weights, pushes = [], []
        for group in groups:
            for side in range(3):
                weight = conv_weight(group, side, target)
                misfit = conv_buf[group, side, conv_obs:, conv_obs : 2 * conv_obs][0:1].astype(F32)
                weights.append(weight)
                pushes.append(weight * misfit)
        spreads = [conv_buf[group, side, :conv_obs, :] for group in groups for side in range(3)]
        flipped = conv_flip[...] if len(groups) == 2 else jnp.concatenate([each.T for each in spreads], axis=1)
        weight, push = (jnp.concatenate(each, axis=1) for each in (weights, pushes))
        add_terms(slot, part, flipped, weight, push, jnp.concatenate(spreads, axis=0), False)

    def add_sat(slot, part, to_chip, side):
        name = (2 * to_chip + core).astype(F32)
        lists = sat_lists[side].astype(F32)
        weight = jnp.where(lists[0:1] == name, 1.0, 0.0) + jnp.where(lists[1:2] == name, 0.5, 0.0)
        add_terms(
            slot, part, sat_flip[side], weight.astype(BF16), weight * lists[2:3], sat_buf[side], side == 0
        )

    has_near = jnp.where(core == 0, chip < chips - 1, chip > 0)
    near = chip + 1 - 2 * core

    def line_copy(way, to_chip, part):
        ahead = block + 2 if way == 0 else block - 2
        span = pl.ds(parts[part].start, parts[part].stop - parts[part].start)
        return pltpu.make_async_remote_copy(
            src_ref=send_buf.at[way, to_chip, span], dst_ref=recv_buf.at[way, to_chip, span],
            send_sem=line_send.at[way, to_chip, part], recv_sem=line_recv.at[way, to_chip, part],
            device_id=(band, ahead), device_id_type=MESH,
        )

    def step_of(way, step):
        if way == 0:
            to_chip = chips - 1 + chip - step
            return to_chip, jnp.logical_and(to_chip > chip, to_chip < chips), has_low
        to_chip = step + chip - chips + 1
        return to_chip, jnp.logical_and(to_chip >= 0, to_chip < chip), has_high

    def finish(way, to_chip, behind, part):
        @pl.when(behind)
        def _():
            line_copy(way, to_chip, part).wait_recv()
            acc[way, parts[part], :] += recv_buf[way, to_chip, parts[part], :].astype(F32)

        send_buf[way, to_chip, part * cut : (part + 1) * cut, :] = acc[
            way, part * cut : (part + 1) * cut, :
        ].astype(BF16)
        if part == 1:
            tail = acc[way, 2 * cut :, :]
            four = [tail[at * lane_blocks : (at + 1) * lane_blocks] for at in range(4)]
            high, kept = (four[at].astype(BF16).astype(F32) for at in (0, 2))
            send_buf[way, to_chip, 2 * cut :, :] = jnp.concatenate(
                [high, four[0] + four[1] - high, kept, four[2] + four[3] - kept], axis=0
            ).astype(BF16)
        line_copy(way, to_chip, part).start()

    loads[6].wait()
    flip_sat(0)
    for way in range(2):
        to_chip, wanted, _ = step_of(way, 0)

        @pl.when(wanted)
        def _():
            for part in range(2):
                add_sat(way, part, to_chip, 0)

    list_copy.wait_recv()
    tile_copy.wait_recv()
    flip_sat(1)

    def step_body(step, carry):
        for part in range(2):
            for way in range(2):
                to_chip, wanted, behind = step_of(way, step)

                @pl.when(wanted)
                def _():
                    @pl.when(step > 0)
                    def _():
                        add_sat(way, part, to_chip, 0)

                    add_sat(way, part, to_chip, 1)

                    @pl.when(to_chip == near)
                    def _():
                        if part == 0:
                            conv_ready()
                        add_conv(way, part, 2 * to_chip + core, (0, 1))

            for way in range(2):
                to_chip, wanted, behind = step_of(way, step)

                @pl.when(wanted)
                def _():
                    finish(way, to_chip, behind, part)

        if chips > 2:
            @pl.when(step == 0)
            def _():
                relay()

        return carry

    if chips == 2:
        relay()

    lax.fori_loop(0, chips - 1, step_body, 0)

    @pl.when(jnp.logical_not(has_near))
    def _():
        conv_ready()

    for part in range(2):
        for side in range(2):
            add_sat(0, part, chip, side)
        add_conv(0, part, block, (0, 1))

    @pl.when(outer)
    def _():
        @pl.when(has_north)
        def _():
            far_south.wait_recv()

        @pl.when(has_south)
        def _():
            far_north.wait_recv()

        for part in range(2):
            add_conv(0, part, block, (2,))

    loads[7].wait()
    ensemble = members_buf[...].astype(F32)
    state_mean = jnp.mean(ensemble, axis=0, keepdims=True)
    anomaly_buf[...] = (ensemble - state_mean).astype(BF16)
    keep = pltpu.make_async_copy(anomaly_buf, anomaly, load.at[8])
    keep.start()
    centre[...] = jnp.broadcast_to(state_mean, centre.shape)

    for part in range(2):
        for way, behind in enumerate((has_low, has_high)):
            @pl.when(behind)
            def _():
                line_copy(way, chip, part).wait_recv()
                acc[0, parts[part], :] += recv_buf[way, chip, parts[part], :].astype(F32)

        out[parts[part], :] = acc[0, parts[part], :]

    keep.wait()
    tile_copy.wait_send()
    list_copy.wait_send()
    to_side.wait_send()

    @pl.when(outer)
    def _():
        around.wait_send()

        @pl.when(has_north)
        def _():
            far_north.wait_send()

        @pl.when(has_south)
        def _():
            far_south.wait_send()

    @pl.when(has_north)
    def _():
        to_north.wait_send()
        relays[0].wait_send()

    @pl.when(has_south)
    def _():
        to_south.wait_send()
        relays[1].wait_send()

    def drain(step, carry):
        for way in range(2):
            to_chip, wanted, _ = step_of(way, step)

            @pl.when(wanted)
            def _():
                for part in range(2):
                    line_copy(way, to_chip, part).wait_send()
        return carry

    lax.fori_loop(0, chips - 1, drain, 0)


def analyse_kernel(
    packed, state_mean, spread, out, anomaly_buf, out_buf, y, u, w, e, f, h, t, load, store
):
    members = spread.shape[0]
    fetch = pltpu.make_async_copy(spread, anomaly_buf, load)
    fetch.start()
    half, lane_blocks = members // 2, members // LANES
    blocks = [packed[at * half : (at + 1) * half] for at in range(lane_blocks)]
    cross = jnp.concatenate(blocks[: lane_blocks // 2], axis=1)
    field = jnp.concatenate(blocks[lane_blocks // 2 :], axis=1)
    tail = packed[lane_blocks * half :]

    def tail_row(first, count):
        at = [first * lane_blocks + each for each in range(count)]
        return jnp.concatenate(
            [tail[each : each + 1] + tail[each + lane_blocks : each + lane_blocks + 1] for each in at], axis=1
        )

    drive = tail_row(0, lane_blocks)
    diagonal = tail_row(2, lane_blocks // 2)
    row, col = iota((half, half), 0), iota((half, half), 1)
    on = row == col
    strict = jnp.where(row < col, field, 0.0)
    under = jnp.where(row > col, field, 0.0)
    first = strict + strict.T + jnp.where(on, field + (members - 1.0), 0.0)
    second = under + under.T + jnp.where(on, diagonal + (members - 1.0), 0.0)
    squares = first * first + second * second + 2.0 * cross * cross
    square_sum = jnp.sum(jnp.sum(squares, axis=0, keepdims=True), axis=1, keepdims=True)
    scale = jnp.sqrt(square_sum)
    shrink = 1.0 / scale
    upper_right = cross * shrink
    y[:half, :half] = (first * shrink).astype(BF16)
    y[half:, half:] = (second * shrink).astype(BF16)
    y[:half, half:] = upper_right.astype(BF16)
    y[half:, :half] = upper_right.T.astype(BF16)

    bands = [slice(at * half, (at + 1) * half) for at in range(2)]
    for band in bands:
        own = y[band, :].astype(F32)
        square = dot(y[band, :], y[...])
        u[band, :] = (1.5 * own - 0.5 * square).astype(BF16)
        w[band, :] = (0.25 * square - 1.5 * own).astype(BF16)
    for band in bands:
        product = dot(u[band, :], w[...])
        e[band, :] = (
            -0.75 * y[band, :].astype(F32) - 1.125 * u[band, :].astype(F32) - 0.5 * product
        ).astype(BF16)
    for band in bands:
        f[band, :] = (2.25 * y[band, :].astype(F32) + dot(y[band, :], e[...])).astype(BF16)
        h[band, :] = (4.5 * e[band, :].astype(F32) + dot(e[band, :], e[...])).astype(BF16)
    for band in bands:
        product = dot(f[band, :], h[...])
        t[band, :] = (
            1.5 * e[band, :].astype(F32) - 2.53125 * f[band, :].astype(F32) - 0.5 * product
        ).astype(BF16)

    def times_root(vector):
        high = vector.astype(BF16)
        low = (vector - high.astype(F32)).astype(BF16)
        place = iota((16, members), 0)
        both = jnp.where(place == 0, high.astype(F32), jnp.where(place == 1, low.astype(F32), 0.0))
        product = dot(both.astype(BF16), t[...])
        return 3.375 * vector + product[0:1] + product[1:2]

    mean_weight = times_root(times_root(drive)) * shrink
    gain = jnp.sqrt((members - 1.0) * shrink)
    fetch.wait()
    part = members // STORES
    stores = [
        pltpu.make_async_copy(
            out_buf.at[pl.ds(at * part, part)], out.at[0, 0, pl.ds(at * part, part)], store.at[at]
        )
        for at in range(STORES)
    ]
    for at, copy in enumerate(stores):
        band = slice(at * part, (at + 1) * part)
        one = iota((part, members), 0) + at * part == iota((part, members), 1)
        root = t[band, :].astype(F32) + jnp.where(one, 3.375, 0.0)
        transform = (gain * root + mean_weight).astype(BF16)
        out_buf[band, :] = dot(transform, anomaly_buf[...]) + state_mean[0:1]
        copy.start()
    for copy in stores:
        copy.wait()


def shards(
    n_lat, n_lon,
    background, conv_pert, conv_misfit, conv_column, sat_pert, sat_misfit, sat_rows, sat_targets,
):
    members, cells = background.shape[2:]
    tiles, tile_obs = sat_pert.shape[1:3]
    conv_obs = conv_pert.shape[2]
    rows, chips, half = tiles * tile_obs, n_lon // 2, members // 2
    vmem = pl.BlockSpec(memory_space=pltpu.VMEM)
    lanes_long = members // LANES * half + EXTRA
    hbm = pl.BlockSpec(memory_space=pltpu.HBM)
    packed, anomaly, state_mean = pl.pallas_call(
        functools.partial(gather_kernel, n_lat, n_lon),
        out_shape=(
            jax.ShapeDtypeStruct((lanes_long, LANES), F32),
            jax.ShapeDtypeStruct((members, cells), BF16),
            jax.ShapeDtypeStruct((8, cells), F32),
        ),
        in_specs=[hbm] * 8,
        out_specs=(vmem, hbm, vmem),
        scratch_shapes=[
            pltpu.VMEM((members, cells), BF16),
            pltpu.VMEM((members, cells), BF16),
            pltpu.VMEM((1, 1, conv_obs), BF16),
            pltpu.VMEM((1, 1, conv_obs), jnp.int32),
            pltpu.VMEM((1, tiles, tile_obs), BF16),
            pltpu.VMEM((1, tiles), jnp.int32),
            pltpu.VMEM((1, 2, tiles), jnp.int32),
            pltpu.VMEM((2, rows, members), BF16),
            pltpu.VMEM((2, EXTRA, rows), BF16),
            pltpu.VMEM((3, 3, conv_obs + EXTRA, members), BF16),
            pltpu.VMEM((2, members, rows), BF16),
            pltpu.VMEM((members, 6 * conv_obs), BF16),
            pltpu.VMEM((2, lanes_long, LANES), F32),
            pltpu.VMEM((2, chips, lanes_long, LANES), BF16),
            pltpu.VMEM((2, chips, lanes_long, LANES), BF16),
            pltpu.SemaphoreType.DMA((9,)),
            pltpu.SemaphoreType.DMA((2,)),
            pltpu.SemaphoreType.DMA((2,)),
            pltpu.SemaphoreType.DMA((8,)),
            pltpu.SemaphoreType.DMA((8,)),
            pltpu.SemaphoreType.DMA((2, chips, 2)),
            pltpu.SemaphoreType.DMA((2, chips, 2)),
        ],
        compiler_params=pltpu.CompilerParams(
            collective_id=0, has_side_effects=True, vmem_limit_bytes=64 * 1024 * 1024
        ),
        cost_estimate=pl.CostEstimate(
            flops=2 * (chips * 2 * rows + 9 * conv_obs) * members * members,
            bytes_accessed=4 * rows * members, transcendentals=0,
        ),
        name="gather_grams",
    )(
        background, conv_pert, conv_misfit, conv_column, sat_pert.reshape(rows, members), sat_misfit, sat_rows,
        jnp.swapaxes(sat_targets, 1, 2),
    )
    return pl.pallas_call(
        analyse_kernel,
        out_shape=jax.ShapeDtypeStruct((1, 1, members, cells), F32),
        in_specs=[vmem, vmem, hbm],
        out_specs=hbm,
        scratch_shapes=[
            pltpu.VMEM((members, cells), BF16),
            pltpu.VMEM((members, cells), F32),
            *[pltpu.VMEM((members, members), BF16)] * 7,
            pltpu.SemaphoreType.DMA,
            pltpu.SemaphoreType.DMA((STORES,)),
        ],
        compiler_params=pltpu.CompilerParams(vmem_limit_bytes=64 * 1024 * 1024),
        cost_estimate=pl.CostEstimate(
            flops=14 * members * members * members, bytes_accessed=6 * members * cells, transcendentals=0
        ),
        name="analyse",
    )(packed, state_mean, anomaly)


def solution(mesh):
    placed = (
        P("lat", "lon", None, None),
        P("lat", "lon", None, None),
        P("lat", "lon", None),
        P("lat", "lon", None),
        P("lat", "lon", None, None),
        P("lat", "lon", None),
        P("lat", "lon"),
        P("lat", "lon", None),
    )
    return jax.shard_map(
        functools.partial(shards, mesh.shape["lat"], mesh.shape["lon"]),
        mesh=mesh, in_specs=placed, out_specs=P("lat", "lon", None, None), check_vma=False,
    )
```

```python
import functools

import jax
import jax.numpy as jnp
from jax import lax
from jax.experimental import pallas as pl
from jax.experimental.pallas import tpu as pltpu
from jax.sharding import PartitionSpec as P

BLK = 16
MESH = pl.DeviceIdType.MESH
F32 = jnp.float32
BF16 = jnp.bfloat16
EXTRA = 16
LANES = 128
STORES = 4


def dot(left, right):
    return lax.dot_general(left, right, (((1,), (0,)), ((), ())), preferred_element_type=F32)


def iota(shape, dim):
    return lax.broadcasted_iota(jnp.int32, shape, dim)


def gather_kernel(
    n_lat, n_lon,
    background, conv_pert, conv_misfit, conv_column, sat_pert, sat_misfit, sat_rows, sat_targets,
    out, anomaly, centre,
    members_buf, anomaly_buf, small_misfit, small_column, tile_misfit, tile_rows, tile_targets,
    sat_buf, sat_lists, conv_buf, sat_flip, conv_flip, acc, send_buf, recv_buf,
    load, sat_send, sat_recv, conv_send, conv_recv, line_send, line_recv,
):
    chips = n_lon // 2
    band = lax.axis_index("lat")
    block = lax.axis_index("lon")
    chip, core = block // 2, block % 2
    sibling = 2 * chip + (1 - core)
    opposite = n_lon - 1 - block
    tiles, tile_obs = sat_misfit.shape[1], sat_misfit.shape[2]
    rows, members = tiles * tile_obs, sat_pert.shape[1]
    conv_obs = conv_pert.shape[2]
    half, lane_blocks = members // 2, members // LANES
    has_north, has_south = band > 0, band < n_lat - 1
    has_low, has_high = chip > 0, chip < chips - 1
    outer = jnp.logical_or(block == 0, block == n_lon - 1)
    mates = (
        (has_north, (band - 1, block)),
        (has_south, (band + 1, block)),
        (has_low, (band, block - 2)),
        (has_high, (band, block + 2)),
        (outer, (band, opposite)),
    )

    barrier = pltpu.get_barrier_semaphore()
    pl.semaphore_signal(barrier, inc=1, device_id=(band, sibling), device_id_type=MESH)
    for here, mate in mates:
        @pl.when(here)
        def _():
            pl.semaphore_signal(barrier, inc=1, device_id=mate, device_id_type=MESH)

    loads = [
        pltpu.make_async_copy(source, target, load.at[at])
        for at, (source, target) in enumerate(
            (
                (conv_pert.at[0, 0], conv_buf.at[0, 1, pl.ds(0, conv_obs)]),
                (conv_misfit, small_misfit),
                (conv_column, small_column),
                (sat_misfit, tile_misfit),
                (sat_rows, tile_rows),
                (sat_targets, tile_targets),
                (sat_pert, sat_buf.at[0]),
                (background.at[0, 0], members_buf),
            )
        )
    ]
    for copy in loads:
        copy.start()
    pl.semaphore_wait(barrier, 1 + sum(here.astype(jnp.int32) for here, _ in mates))

    def sat_copy(source, target, at):
        return pltpu.make_async_remote_copy(
            src_ref=source, dst_ref=target, send_sem=sat_send.at[at], recv_sem=sat_recv.at[at],
            device_id=(band, sibling), device_id_type=MESH,
        )

    spans = [pl.ds(at * (rows // 2), rows // 2) for at in range(2)]
    tile_copies = [sat_copy(sat_pert.at[span], sat_buf.at[1, span], at) for at, span in enumerate(spans)]
    list_copy = sat_copy(sat_lists.at[0], sat_lists.at[1], 2)
    for copy in tile_copies:
        copy.start()

    for copy in loads[:6]:
        copy.wait()
    conv_buf[0, 1, conv_obs:, :] = jnp.concatenate(
        [
            jnp.broadcast_to(small_column[0].astype(F32).astype(BF16), (EXTRA, conv_obs)),
            jnp.broadcast_to(small_misfit[0], (EXTRA, conv_obs)),
            jnp.zeros((EXTRA, members - 2 * conv_obs), BF16),
        ],
        axis=1,
    )

    def conv_copy(group, slot, to_group, to_slot, sem, mate):
        return pltpu.make_async_remote_copy(
            src_ref=conv_buf.at[group, slot], dst_ref=conv_buf.at[to_group, to_slot],
            send_sem=conv_send.at[sem], recv_sem=conv_recv.at[sem],
            device_id=mate, device_id_type=MESH,
        )

    to_north = conv_copy(0, 1, 0, 2, 0, (band - 1, block))
    to_south = conv_copy(0, 1, 0, 0, 1, (band + 1, block))
    to_side = conv_copy(0, 1, 1, 1, 2, (band, sibling))
    relays = [conv_copy(0, 0, 1, 0, 3, (band, sibling)), conv_copy(0, 2, 1, 2, 4, (band, sibling))]
    around = conv_copy(0, 1, 2, 1, 5, (band, opposite))
    far_north = conv_copy(2, 1, 2, 2, 6, (band - 1, block))
    far_south = conv_copy(2, 1, 2, 0, 7, (band + 1, block))

    @pl.when(outer)
    def _():
        around.start()

    @pl.when(has_north)
    def _():
        to_north.start()

    @pl.when(has_south)
    def _():
        to_south.start()

    own_tile = iota((tiles, rows), 1) // tile_obs == iota((tiles, rows), 0)
    own_mask = own_tile.astype(BF16)
    spread_obs = (iota((tile_obs, rows), 1) % tile_obs == iota((tile_obs, rows), 0)).astype(BF16)
    misfit = jnp.sum(jnp.where(own_tile, dot(tile_misfit[0], spread_obs), 0.0), axis=0, keepdims=True)
    count = dot(jnp.broadcast_to(tile_rows[...].astype(F32).astype(BF16), (8, tiles)), own_mask)[0:1]
    live = (iota((1, rows), 1) % tile_obs).astype(F32) < count
    names = tile_targets[0].astype(F32)
    lists = [
        jnp.where(
            live,
            dot(jnp.broadcast_to(names[e : e + 1], (8, tiles)).astype(BF16), own_mask)[0:1],
            -1.0,
        )
        for e in range(2)
    ]
    place = iota((EXTRA, rows), 0)
    sat_lists[0] = jnp.where(
        place == 0, lists[0], jnp.where(place == 1, lists[1], jnp.where(place == 2, misfit, 0.0))
    ).astype(BF16)
    list_copy.start()
    to_side.start()

    def flip_sat(side, part, span):
        lanes = slice(part * half, (part + 1) * half)
        sat_flip[side, lanes, span] = sat_buf[side, span, lanes].T

    def relay():
        blank = jnp.zeros((conv_obs + EXTRA, members), BF16)

        @pl.when(jnp.logical_not(has_north))
        def _():
            for group in range(3):
                conv_buf[group, 0] = blank

        @pl.when(jnp.logical_not(has_south))
        def _():
            for group in range(3):
                conv_buf[group, 2] = blank

        @pl.when(has_north)
        def _():
            to_south.wait_recv()
            relays[0].start()

        @pl.when(has_south)
        def _():
            to_north.wait_recv()
            relays[1].start()

        @pl.when(outer)
        def _():
            around.wait_recv()

            @pl.when(has_north)
            def _():
                far_north.start()

            @pl.when(has_south)
            def _():
                far_south.start()

    def conv_ready():
        to_side.wait_recv()

        @pl.when(has_north)
        def _():
            relays[0].wait_recv()

        @pl.when(has_south)
        def _():
            relays[1].wait_recv()

        for group in range(2):
            for slot in range(3):
                at = (group * 3 + slot) * conv_obs
                conv_flip[:, at : at + conv_obs] = conv_buf[group, slot, :conv_obs, :].T

    def conv_weight(group, slot, target):
        column = conv_buf[group, slot, conv_obs:, :conv_obs][0:1].astype(F32)
        source = (block, sibling, opposite)[group]
        away = lax.rem(source - target + 1 + n_lon, n_lon) - 1
        row = jnp.floor(column * (1.0 / BLK))
        lat_place = BLK * (slot - 1.0) + row + 0.5 - 0.5 * BLK
        lon_place = BLK * away.astype(F32) + (column - BLK * row) + 0.5 - 0.5 * BLK
        weight = jnp.exp(-(lat_place * lat_place + lon_place * lon_place) / (2.0 * BLK * BLK))
        return jnp.where(away <= 1, weight, 0.0)

    place = iota((EXTRA, LANES), 0)
    eye = iota((half, half), 0) == iota((half, half), 1)
    upper = iota((half, half), 0) <= iota((half, half), 1)

    cut = lane_blocks // 2 * half
    parts = (slice(0, cut), slice(cut, 2 * cut + EXTRA))

    def add_terms(slot, part, flipped, weight, push, spread, first):
        def put(into, term):
            if first:
                acc[slot, into, :] = term
            else:
                acc[slot, into, :] += term

        def scaled(rows_of):
            if weight.dtype == BF16:
                return rows_of * weight
            return (rows_of.astype(F32) * weight).astype(BF16)

        if part == 0:
            piece = dot(scaled(flipped[:half]), spread[:, half:])
        else:
            low = dot(scaled(flipped[half:]), spread[:, half:])
            piece = jnp.where(upper, dot(scaled(flipped[:half]), spread[:, :half]), low)
            drive = dot(jnp.broadcast_to(push, (EXTRA, push.shape[1])).astype(BF16), spread)
            diagonal = jnp.sum(jnp.where(eye, low, 0.0), axis=0, keepdims=True)
            tail = jnp.zeros((EXTRA, LANES), F32)
            for at in range(lane_blocks):
                lanes = slice(at * LANES, (at + 1) * LANES)
                tail += jnp.where(place == at, drive[0:1, lanes], 0.0)
                if at < lane_blocks // 2:
                    tail += jnp.where(place == 2 * lane_blocks + at, diagonal[:, lanes], 0.0)
            put(slice(2 * cut, 2 * cut + EXTRA), tail)
        for at in range(lane_blocks // 2):
            put(slice(part * cut + at * half, part * cut + (at + 1) * half), piece[:, at * LANES : (at + 1) * LANES])

    def add_conv(slot, part, target, groups):
        weights, pushes = [], []
        for group in groups:
            for side in range(3):
                weight = conv_weight(group, side, target)
                misfit = conv_buf[group, side, conv_obs:, conv_obs : 2 * conv_obs][0:1].astype(F32)
                weights.append(weight)
                pushes.append(weight * misfit)
        spreads = [conv_buf[group, side, :conv_obs, :] for group in groups for side in range(3)]
        flipped = conv_flip[...] if len(groups) == 2 else jnp.concatenate([each.T for each in spreads], axis=1)
        weight, push = (jnp.concatenate(each, axis=1) for each in (weights, pushes))
        add_terms(slot, part, flipped, weight, push, jnp.concatenate(spreads, axis=0), False)

    def add_sat(slot, part, to_chip, side):
        name = (2 * to_chip + core).astype(F32)
        lists = sat_lists[side].astype(F32)
        weight = jnp.where(lists[0:1] == name, 1.0, 0.0) + jnp.where(lists[1:2] == name, 0.5, 0.0)
        add_terms(
            slot, part, sat_flip[side], weight.astype(BF16), weight * lists[2:3], sat_buf[side], side == 0
        )

    has_near = jnp.where(core == 0, chip < chips - 1, chip > 0)
    near = chip + 1 - 2 * core

    def line_copy(way, to_chip, part):
        ahead = block + 2 if way == 0 else block - 2
        span = pl.ds(parts[part].start, parts[part].stop - parts[part].start)
        return pltpu.make_async_remote_copy(
            src_ref=send_buf.at[way, to_chip, span], dst_ref=recv_buf.at[way, to_chip, span],
            send_sem=line_send.at[way, to_chip, part], recv_sem=line_recv.at[way, to_chip, part],
            device_id=(band, ahead), device_id_type=MESH,
        )

    def step_of(way, step):
        if way == 0:
            to_chip = chips - 1 + chip - step
            return to_chip, jnp.logical_and(to_chip > chip, to_chip < chips), has_low
        to_chip = step + chip - chips + 1
        return to_chip, jnp.logical_and(to_chip >= 0, to_chip < chip), has_high

    def finish(way, to_chip, behind, part):
        @pl.when(behind)
        def _():
            line_copy(way, to_chip, part).wait_recv()
            acc[way, parts[part], :] += recv_buf[way, to_chip, parts[part], :].astype(F32)

        send_buf[way, to_chip, part * cut : (part + 1) * cut, :] = acc[
            way, part * cut : (part + 1) * cut, :
        ].astype(BF16)
        if part == 1:
            tail = acc[way, 2 * cut :, :]
            four = [tail[at * lane_blocks : (at + 1) * lane_blocks] for at in range(4)]
            high, kept = (four[at].astype(BF16).astype(F32) for at in (0, 2))
            send_buf[way, to_chip, 2 * cut :, :] = jnp.concatenate(
                [high, four[0] + four[1] - high, kept, four[2] + four[3] - kept], axis=0
            ).astype(BF16)
        line_copy(way, to_chip, part).start()

    loads[6].wait()
    for span in spans:
        flip_sat(0, 0, span)
    for way in range(2):
        to_chip, wanted, _ = step_of(way, 0)

        @pl.when(wanted)
        def _():
            add_sat(way, 0, to_chip, 0)

    list_copy.wait_recv()
    for copy, span in zip(tile_copies, spans):
        copy.wait_recv()
        flip_sat(1, 0, span)

    def step_body(step, carry):
        for part in range(2):
            if part == 1:
                @pl.when(step == 0)
                def _():
                    for side in range(2):
                        for span in spans:
                            flip_sat(side, 1, span)

            for way in range(2):
                to_chip, wanted, behind = step_of(way, step)

                @pl.when(wanted)
                def _():
                    @pl.when(jnp.logical_or(step > 0, part == 1))
                    def _():
                        add_sat(way, part, to_chip, 0)

                    add_sat(way, part, to_chip, 1)

                    @pl.when(to_chip == near)
                    def _():
                        if part == 0:
                            conv_ready()
                        add_conv(way, part, 2 * to_chip + core, (0, 1))

            for way in range(2):
                to_chip, wanted, behind = step_of(way, step)

                @pl.when(wanted)
                def _():
                    finish(way, to_chip, behind, part)

        if chips > 2:
            @pl.when(step == 0)
            def _():
                relay()

        return carry

    if chips == 2:
        relay()

    lax.fori_loop(0, chips - 1, step_body, 0)

    @pl.when(jnp.logical_not(has_near))
    def _():
        conv_ready()

    for part in range(2):
        for side in range(2):
            add_sat(0, part, chip, side)
        add_conv(0, part, block, (0, 1))

    @pl.when(outer)
    def _():
        @pl.when(has_north)
        def _():
            far_south.wait_recv()

        @pl.when(has_south)
        def _():
            far_north.wait_recv()

        for part in range(2):
            add_conv(0, part, block, (2,))

    loads[7].wait()
    ensemble = members_buf[...].astype(F32)
    state_mean = jnp.mean(ensemble, axis=0, keepdims=True)
    anomaly_buf[...] = (ensemble - state_mean).astype(BF16)
    keep = pltpu.make_async_copy(anomaly_buf, anomaly, load.at[8])
    keep.start()
    centre[...] = jnp.broadcast_to(state_mean, centre.shape)

    for part in range(2):
        for way, behind in enumerate((has_low, has_high)):
            @pl.when(behind)
            def _():
                line_copy(way, chip, part).wait_recv()
                acc[0, parts[part], :] += recv_buf[way, chip, parts[part], :].astype(F32)

        out[parts[part], :] = acc[0, parts[part], :]

    keep.wait()
    for copy in tile_copies:
        copy.wait_send()
    list_copy.wait_send()
    to_side.wait_send()

    @pl.when(outer)
    def _():
        around.wait_send()

        @pl.when(has_north)
        def _():
            far_north.wait_send()

        @pl.when(has_south)
        def _():
            far_south.wait_send()

    @pl.when(has_north)
    def _():
        to_north.wait_send()
        relays[0].wait_send()

    @pl.when(has_south)
    def _():
        to_south.wait_send()
        relays[1].wait_send()

    def drain(step, carry):
        for way in range(2):
            to_chip, wanted, _ = step_of(way, step)

            @pl.when(wanted)
            def _():
                for part in range(2):
                    line_copy(way, to_chip, part).wait_send()
        return carry

    lax.fori_loop(0, chips - 1, drain, 0)


def analyse_kernel(
    packed, state_mean, spread, out, anomaly_buf, out_buf, y, u, w, e, f, h, t, load, store
):
    members = spread.shape[0]
    fetch = pltpu.make_async_copy(spread, anomaly_buf, load)
    fetch.start()
    half, lane_blocks = members // 2, members // LANES
    blocks = [packed[at * half : (at + 1) * half] for at in range(lane_blocks)]
    cross = jnp.concatenate(blocks[: lane_blocks // 2], axis=1)
    field = jnp.concatenate(blocks[lane_blocks // 2 :], axis=1)
    tail = packed[lane_blocks * half :]

    def tail_row(first, count):
        at = [first * lane_blocks + each for each in range(count)]
        return jnp.concatenate(
            [tail[each : each + 1] + tail[each + lane_blocks : each + lane_blocks + 1] for each in at], axis=1
        )

    drive = tail_row(0, lane_blocks)
    diagonal = tail_row(2, lane_blocks // 2)
    row, col = iota((half, half), 0), iota((half, half), 1)
    on = row == col
    turned = field.T
    first = jnp.where(row < col, field, turned) + jnp.where(on, members - 1.0, 0.0)
    second = jnp.where(on, diagonal + (members - 1.0), jnp.where(row > col, field, turned))
    lone = diagonal + (members - 1.0)
    apart = jnp.where(on, 0.0, field)
    kept = field + (members - 1.0)
    squares = 2.0 * (apart * apart + cross * cross) + jnp.where(on, kept * kept, 0.0)
    square_sum = jnp.sum(
        jnp.sum(squares, axis=0, keepdims=True) + lone * lone, axis=1, keepdims=True
    )
    scale = jnp.sqrt(square_sum)
    shrink = 1.0 / scale
    upper_right = cross * shrink
    y[:half, :half] = (first * shrink).astype(BF16)
    y[half:, half:] = (second * shrink).astype(BF16)
    y[:half, half:] = upper_right.astype(BF16)
    y[half:, :half] = upper_right.T.astype(BF16)

    bands = [slice(at * half, (at + 1) * half) for at in range(2)]
    for band in bands:
        own = y[band, :].astype(F32)
        square = dot(y[band, :], y[...])
        u[band, :] = (1.5 * own - 0.5 * square).astype(BF16)
        w[band, :] = (0.25 * square - 1.5 * own).astype(BF16)
    for band in bands:
        product = dot(u[band, :], w[...])
        e[band, :] = (
            -0.75 * y[band, :].astype(F32) - 1.125 * u[band, :].astype(F32) - 0.5 * product
        ).astype(BF16)
    for band in bands:
        f[band, :] = (2.25 * y[band, :].astype(F32) + dot(y[band, :], e[...])).astype(BF16)
        h[band, :] = (4.5 * e[band, :].astype(F32) + dot(e[band, :], e[...])).astype(BF16)
    def times(vector, matrix):
        high = vector.astype(BF16)
        low = (vector - high.astype(F32)).astype(BF16)
        place = iota((16, members), 0)
        both = jnp.where(place == 0, high.astype(F32), jnp.where(place == 1, low.astype(F32), 0.0))
        product = dot(both.astype(BF16), matrix[...])
        return product[0:1] + product[1:2]

    drive_f = times(drive, f)
    push = 3.375 * drive + 1.5 * times(drive, e) - 2.53125 * drive_f - 0.5 * times(drive_f, h)
    for band in bands:
        product = dot(f[band, :], h[...])
        t[band, :] = (
            1.5 * e[band, :].astype(F32) - 2.53125 * f[band, :].astype(F32) - 0.5 * product
        ).astype(BF16)
    mean_weight = (3.375 * push + times(push, t)) * shrink
    gain = jnp.sqrt((members - 1.0) * shrink)
    fetch.wait()
    part = members // STORES
    stores = [
        pltpu.make_async_copy(
            out_buf.at[pl.ds(at * part, part)], out.at[0, 0, pl.ds(at * part, part)], store.at[at]
        )
        for at in range(STORES)
    ]
    for at, copy in enumerate(stores):
        band = slice(at * part, (at + 1) * part)
        one = iota((part, members), 0) + at * part == iota((part, members), 1)
        root = t[band, :].astype(F32) + jnp.where(one, 3.375, 0.0)
        transform = (gain * root + mean_weight).astype(BF16)
        out_buf[band, :] = dot(transform, anomaly_buf[...]) + state_mean[0:1]
        copy.start()
    for copy in stores:
        copy.wait()


def shards(
    n_lat, n_lon,
    background, conv_pert, conv_misfit, conv_column, sat_pert, sat_misfit, sat_rows, sat_targets,
):
    members, cells = background.shape[2:]
    tiles, tile_obs = sat_pert.shape[1:3]
    conv_obs = conv_pert.shape[2]
    rows, chips, half = tiles * tile_obs, n_lon // 2, members // 2
    vmem = pl.BlockSpec(memory_space=pltpu.VMEM)
    lanes_long = members // LANES * half + EXTRA
    hbm = pl.BlockSpec(memory_space=pltpu.HBM)
    packed, anomaly, state_mean = pl.pallas_call(
        functools.partial(gather_kernel, n_lat, n_lon),
        out_shape=(
            jax.ShapeDtypeStruct((lanes_long, LANES), F32),
            jax.ShapeDtypeStruct((members, cells), BF16),
            jax.ShapeDtypeStruct((8, cells), F32),
        ),
        in_specs=[hbm] * 8,
        out_specs=(vmem, hbm, vmem),
        scratch_shapes=[
            pltpu.VMEM((members, cells), BF16),
            pltpu.VMEM((members, cells), BF16),
            pltpu.VMEM((1, 1, conv_obs), BF16),
            pltpu.VMEM((1, 1, conv_obs), jnp.int32),
            pltpu.VMEM((1, tiles, tile_obs), BF16),
            pltpu.VMEM((1, tiles), jnp.int32),
            pltpu.VMEM((1, 2, tiles), jnp.int32),
            pltpu.VMEM((2, rows, members), BF16),
            pltpu.VMEM((2, EXTRA, rows), BF16),
            pltpu.VMEM((3, 3, conv_obs + EXTRA, members), BF16),
            pltpu.VMEM((2, members, rows), BF16),
            pltpu.VMEM((members, 6 * conv_obs), BF16),
            pltpu.VMEM((2, lanes_long, LANES), F32),
            pltpu.VMEM((2, chips, lanes_long, LANES), BF16),
            pltpu.VMEM((2, chips, lanes_long, LANES), BF16),
            pltpu.SemaphoreType.DMA((9,)),
            pltpu.SemaphoreType.DMA((3,)),
            pltpu.SemaphoreType.DMA((3,)),
            pltpu.SemaphoreType.DMA((8,)),
            pltpu.SemaphoreType.DMA((8,)),
            pltpu.SemaphoreType.DMA((2, chips, 2)),
            pltpu.SemaphoreType.DMA((2, chips, 2)),
        ],
        compiler_params=pltpu.CompilerParams(
            collective_id=0, has_side_effects=True, vmem_limit_bytes=64 * 1024 * 1024
        ),
        cost_estimate=pl.CostEstimate(
            flops=2 * (chips * 2 * rows + 9 * conv_obs) * members * members,
            bytes_accessed=4 * rows * members, transcendentals=0,
        ),
        name="gather_grams",
    )(
        background, conv_pert, conv_misfit, conv_column, sat_pert.reshape(rows, members), sat_misfit, sat_rows,
        jnp.swapaxes(sat_targets, 1, 2),
    )
    return pl.pallas_call(
        analyse_kernel,
        out_shape=jax.ShapeDtypeStruct((1, 1, members, cells), F32),
        in_specs=[vmem, vmem, hbm],
        out_specs=hbm,
        scratch_shapes=[
            pltpu.VMEM((members, cells), BF16),
            pltpu.VMEM((members, cells), F32),
            *[pltpu.VMEM((members, members), BF16)] * 7,
            pltpu.SemaphoreType.DMA,
            pltpu.SemaphoreType.DMA((STORES,)),
        ],
        compiler_params=pltpu.CompilerParams(vmem_limit_bytes=64 * 1024 * 1024),
        cost_estimate=pl.CostEstimate(
            flops=14 * members * members * members, bytes_accessed=6 * members * cells, transcendentals=0
        ),
        name="analyse",
    )(packed, state_mean, anomaly)


def solution(mesh):
    placed = (
        P("lat", "lon", None, None),
        P("lat", "lon", None, None),
        P("lat", "lon", None),
        P("lat", "lon", None),
        P("lat", "lon", None, None),
        P("lat", "lon", None),
        P("lat", "lon"),
        P("lat", "lon", None),
    )
    return jax.shard_map(
        functools.partial(shards, mesh.shape["lat"], mesh.shape["lon"]),
        mesh=mesh, in_specs=placed, out_specs=P("lat", "lon", None, None), check_vma=False,
    )
```

```python
import functools

import jax
import jax.numpy as jnp
from jax import lax
from jax.experimental import pallas as pl
from jax.experimental.pallas import tpu as pltpu
from jax.sharding import PartitionSpec as P

BLK = 16
MESH = pl.DeviceIdType.MESH
F32 = jnp.float32
BF16 = jnp.bfloat16
EXTRA = 16
LANES = 128
STORES = 4


def dot(left, right):
    return lax.dot_general(left, right, (((1,), (0,)), ((), ())), preferred_element_type=F32)


def iota(shape, dim):
    return lax.broadcasted_iota(jnp.int32, shape, dim)


def gather_kernel(
    n_lat, n_lon,
    background, conv_pert, conv_misfit, conv_column, sat_pert, sat_misfit, sat_rows, sat_targets,
    out, anomaly, centre,
    members_buf, anomaly_buf, small_misfit, small_column, tile_misfit, tile_rows, tile_targets,
    sat_buf, sat_lists, conv_buf, sat_flip, conv_flip, acc, send_buf, recv_buf,
    load, sat_send, sat_recv, conv_send, conv_recv, line_send, line_recv,
):
    chips = n_lon // 2
    band = lax.axis_index("lat")
    block = lax.axis_index("lon")
    chip, core = block // 2, block % 2
    sibling = 2 * chip + (1 - core)
    opposite = n_lon - 1 - block
    tiles, tile_obs = sat_misfit.shape[1], sat_misfit.shape[2]
    rows, members = tiles * tile_obs, sat_pert.shape[1]
    conv_obs = conv_pert.shape[2]
    half, lane_blocks = members // 2, members // LANES
    has_north, has_south = band > 0, band < n_lat - 1
    has_low, has_high = chip > 0, chip < chips - 1
    outer = jnp.logical_or(block == 0, block == n_lon - 1)
    mates = (
        (has_north, (band - 1, block)),
        (has_south, (band + 1, block)),
        (has_low, (band, block - 2)),
        (has_high, (band, block + 2)),
        (outer, (band, opposite)),
    )

    barrier = pltpu.get_barrier_semaphore()
    pl.semaphore_signal(barrier, inc=1, device_id=(band, sibling), device_id_type=MESH)
    for here, mate in mates:
        @pl.when(here)
        def _():
            pl.semaphore_signal(barrier, inc=1, device_id=mate, device_id_type=MESH)

    loads = [
        pltpu.make_async_copy(source, target, load.at[at])
        for at, (source, target) in enumerate(
            (
                (conv_pert.at[0, 0], conv_buf.at[0, 1, pl.ds(0, conv_obs)]),
                (conv_misfit, small_misfit),
                (conv_column, small_column),
                (sat_misfit, tile_misfit),
                (sat_rows, tile_rows),
                (sat_targets, tile_targets),
                (sat_pert, sat_buf.at[0]),
                (background.at[0, 0], members_buf),
            )
        )
    ]
    for copy in loads:
        copy.start()
    pl.semaphore_wait(barrier, 1 + sum(here.astype(jnp.int32) for here, _ in mates))

    def sat_copy(source, target, at):
        return pltpu.make_async_remote_copy(
            src_ref=source, dst_ref=target, send_sem=sat_send.at[at], recv_sem=sat_recv.at[at],
            device_id=(band, sibling), device_id_type=MESH,
        )

    spans = [pl.ds(at * (rows // 2), rows // 2) for at in range(2)]
    tile_copies = [sat_copy(sat_pert.at[span], sat_buf.at[1, span], at) for at, span in enumerate(spans)]
    list_copy = sat_copy(sat_lists.at[0], sat_lists.at[1], 2)
    for copy in tile_copies:
        copy.start()

    for copy in loads[:6]:
        copy.wait()
    conv_buf[0, 1, conv_obs:, :] = jnp.concatenate(
        [
            jnp.broadcast_to(small_column[0].astype(F32).astype(BF16), (EXTRA, conv_obs)),
            jnp.broadcast_to(small_misfit[0], (EXTRA, conv_obs)),
            jnp.zeros((EXTRA, members - 2 * conv_obs), BF16),
        ],
        axis=1,
    )

    def conv_copy(group, slot, to_group, to_slot, sem, mate):
        return pltpu.make_async_remote_copy(
            src_ref=conv_buf.at[group, slot], dst_ref=conv_buf.at[to_group, to_slot],
            send_sem=conv_send.at[sem], recv_sem=conv_recv.at[sem],
            device_id=mate, device_id_type=MESH,
        )

    to_north = conv_copy(0, 1, 0, 2, 0, (band - 1, block))
    to_south = conv_copy(0, 1, 0, 0, 1, (band + 1, block))
    to_side = conv_copy(0, 1, 1, 1, 2, (band, sibling))
    relays = [conv_copy(0, 0, 1, 0, 3, (band, sibling)), conv_copy(0, 2, 1, 2, 4, (band, sibling))]
    around = conv_copy(0, 1, 2, 1, 5, (band, opposite))
    far_north = conv_copy(2, 1, 2, 2, 6, (band - 1, block))
    far_south = conv_copy(2, 1, 2, 0, 7, (band + 1, block))

    @pl.when(outer)
    def _():
        around.start()

    @pl.when(has_north)
    def _():
        to_north.start()

    @pl.when(has_south)
    def _():
        to_south.start()

    own_tile = iota((tiles, rows), 1) // tile_obs == iota((tiles, rows), 0)
    own_mask = own_tile.astype(BF16)
    spread_obs = (iota((tile_obs, rows), 1) % tile_obs == iota((tile_obs, rows), 0)).astype(BF16)
    misfit = jnp.sum(jnp.where(own_tile, dot(tile_misfit[0], spread_obs), 0.0), axis=0, keepdims=True)
    count = dot(jnp.broadcast_to(tile_rows[...].astype(F32).astype(BF16), (8, tiles)), own_mask)[0:1]
    live = (iota((1, rows), 1) % tile_obs).astype(F32) < count
    names = tile_targets[0].astype(F32)
    lists = [
        jnp.where(
            live,
            dot(jnp.broadcast_to(names[e : e + 1], (8, tiles)).astype(BF16), own_mask)[0:1],
            -1.0,
        )
        for e in range(2)
    ]
    place = iota((EXTRA, rows), 0)
    sat_lists[0] = jnp.where(
        place == 0, lists[0], jnp.where(place == 1, lists[1], jnp.where(place == 2, misfit, 0.0))
    ).astype(BF16)
    list_copy.start()
    to_side.start()

    def flip_sat(side, part, span):
        lanes = slice(part * half, (part + 1) * half)
        sat_flip[side, lanes, span] = sat_buf[side, span, lanes].T

    def relay():
        blank = jnp.zeros((conv_obs + EXTRA, members), BF16)

        @pl.when(jnp.logical_not(has_north))
        def _():
            for group in range(3):
                conv_buf[group, 0] = blank

        @pl.when(jnp.logical_not(has_south))
        def _():
            for group in range(3):
                conv_buf[group, 2] = blank

        @pl.when(has_north)
        def _():
            to_south.wait_recv()
            relays[0].start()

        @pl.when(has_south)
        def _():
            to_north.wait_recv()
            relays[1].start()

        @pl.when(outer)
        def _():
            around.wait_recv()

            @pl.when(has_north)
            def _():
                far_north.start()

            @pl.when(has_south)
            def _():
                far_south.start()

    def conv_ready():
        to_side.wait_recv()

        @pl.when(has_north)
        def _():
            relays[0].wait_recv()

        @pl.when(has_south)
        def _():
            relays[1].wait_recv()

        for group in range(2):
            for slot in range(3):
                at = (group * 3 + slot) * conv_obs
                conv_flip[:, at : at + conv_obs] = conv_buf[group, slot, :conv_obs, :].T

    def conv_weight(group, slot, target):
        column = conv_buf[group, slot, conv_obs:, :conv_obs][0:1].astype(F32)
        source = (block, sibling, opposite)[group]
        away = lax.rem(source - target + 1 + n_lon, n_lon) - 1
        row = jnp.floor(column * (1.0 / BLK))
        lat_place = BLK * (slot - 1.0) + row + 0.5 - 0.5 * BLK
        lon_place = BLK * away.astype(F32) + (column - BLK * row) + 0.5 - 0.5 * BLK
        weight = jnp.exp(-(lat_place * lat_place + lon_place * lon_place) / (2.0 * BLK * BLK))
        return jnp.where(away <= 1, weight, 0.0)

    place = iota((EXTRA, LANES), 0)
    eye = iota((half, half), 0) == iota((half, half), 1)
    upper = iota((half, half), 0) <= iota((half, half), 1)

    cut = lane_blocks // 2 * half
    parts = (slice(0, cut), slice(cut, 2 * cut + EXTRA))

    def add_terms(slot, part, flipped, weight, push, spread, first):
        def put(into, term):
            if first:
                acc[slot, into, :] = term
            else:
                acc[slot, into, :] += term

        def scaled(rows_of):
            if weight.dtype == BF16:
                return rows_of * weight
            return (rows_of.astype(F32) * weight).astype(BF16)

        if part == 0:
            piece = dot(scaled(flipped[:half]), spread[:, half:])
        else:
            low = dot(scaled(flipped[half:]), spread[:, half:])
            piece = jnp.where(upper, dot(scaled(flipped[:half]), spread[:, :half]), low)
            drive = dot(jnp.broadcast_to(push, (EXTRA, push.shape[1])).astype(BF16), spread)
            diagonal = jnp.sum(jnp.where(eye, low, 0.0), axis=0, keepdims=True)
            tail = jnp.zeros((EXTRA, LANES), F32)
            for at in range(lane_blocks):
                lanes = slice(at * LANES, (at + 1) * LANES)
                tail += jnp.where(place == at, drive[0:1, lanes], 0.0)
                if at < lane_blocks // 2:
                    tail += jnp.where(place == 2 * lane_blocks + at, diagonal[:, lanes], 0.0)
            put(slice(2 * cut, 2 * cut + EXTRA), tail)
        for at in range(lane_blocks // 2):
            put(slice(part * cut + at * half, part * cut + (at + 1) * half), piece[:, at * LANES : (at + 1) * LANES])

    def add_conv(slot, part, target, groups):
        weights, pushes = [], []
        for group in groups:
            for side in range(3):
                weight = conv_weight(group, side, target)
                misfit = conv_buf[group, side, conv_obs:, conv_obs : 2 * conv_obs][0:1].astype(F32)
                weights.append(weight)
                pushes.append(weight * misfit)
        spreads = [conv_buf[group, side, :conv_obs, :] for group in groups for side in range(3)]
        flipped = conv_flip[...] if len(groups) == 2 else jnp.concatenate([each.T for each in spreads], axis=1)
        weight, push = (jnp.concatenate(each, axis=1) for each in (weights, pushes))
        add_terms(slot, part, flipped, weight, push, jnp.concatenate(spreads, axis=0), False)

    def add_sat(slot, part, to_chip, side):
        name = (2 * to_chip + core).astype(F32)
        lists = sat_lists[side].astype(F32)
        weight = jnp.where(lists[0:1] == name, 1.0, 0.0) + jnp.where(lists[1:2] == name, 0.5, 0.0)
        add_terms(
            slot, part, sat_flip[side], weight.astype(BF16), weight * lists[2:3], sat_buf[side], side == 0
        )

    has_near = jnp.where(core == 0, chip < chips - 1, chip > 0)
    near = chip + 1 - 2 * core

    def line_copy(way, to_chip, part):
        ahead = block + 2 if way == 0 else block - 2
        span = pl.ds(parts[part].start, parts[part].stop - parts[part].start)
        return pltpu.make_async_remote_copy(
            src_ref=send_buf.at[way, to_chip, span], dst_ref=recv_buf.at[way, to_chip, span],
            send_sem=line_send.at[way, to_chip, part], recv_sem=line_recv.at[way, to_chip, part],
            device_id=(band, ahead), device_id_type=MESH,
        )

    def step_of(way, step):
        if way == 0:
            to_chip = chips - 1 + chip - step
            return to_chip, jnp.logical_and(to_chip > chip, to_chip < chips), has_low
        to_chip = step + chip - chips + 1
        return to_chip, jnp.logical_and(to_chip >= 0, to_chip < chip), has_high

    def finish(way, to_chip, behind, part):
        @pl.when(behind)
        def _():
            line_copy(way, to_chip, part).wait_recv()
            acc[way, parts[part], :] += recv_buf[way, to_chip, parts[part], :].astype(F32)

        send_buf[way, to_chip, part * cut : (part + 1) * cut, :] = acc[
            way, part * cut : (part + 1) * cut, :
        ].astype(BF16)
        if part == 1:
            tail = acc[way, 2 * cut :, :]
            four = [tail[at * lane_blocks : (at + 1) * lane_blocks] for at in range(4)]
            high, kept = (four[at].astype(BF16).astype(F32) for at in (0, 2))
            send_buf[way, to_chip, 2 * cut :, :] = jnp.concatenate(
                [high, four[0] + four[1] - high, kept, four[2] + four[3] - kept], axis=0
            ).astype(BF16)
        line_copy(way, to_chip, part).start()

    loads[6].wait()
    for span in spans:
        flip_sat(0, 0, span)
    for way in range(2):
        to_chip, wanted, _ = step_of(way, 0)

        @pl.when(wanted)
        def _():
            add_sat(way, 0, to_chip, 0)

    list_copy.wait_recv()
    for copy, span in zip(tile_copies, spans):
        copy.wait_recv()
        flip_sat(1, 0, span)

    keep = pltpu.make_async_copy(anomaly_buf, anomaly, load.at[8])

    own_step = jnp.where(jnp.logical_and(has_low, has_high), 0, chips - 2)

    def own_terms():
        for part in range(2):
            for side in range(2):
                add_sat(2, part, chip, side)
        loads[7].wait()
        ensemble = members_buf[...].astype(F32)
        state_mean = jnp.mean(ensemble, axis=0, keepdims=True)
        anomaly_buf[...] = (ensemble - state_mean).astype(BF16)
        keep.start()
        centre[...] = jnp.broadcast_to(state_mean, centre.shape)

    def step_body(step, carry):
        for part in range(2):
            if part == 1:
                @pl.when(step == 0)
                def _():
                    for side in range(2):
                        for span in spans:
                            flip_sat(side, 1, span)

            for way in range(2):
                to_chip, wanted, behind = step_of(way, step)

                @pl.when(wanted)
                def _():
                    @pl.when(jnp.logical_or(step > 0, part == 1))
                    def _():
                        add_sat(way, part, to_chip, 0)

                    add_sat(way, part, to_chip, 1)

                    @pl.when(to_chip == near)
                    def _():
                        if part == 0:
                            conv_ready()
                        add_conv(way, part, 2 * to_chip + core, (0, 1))

            for way in range(2):
                to_chip, wanted, behind = step_of(way, step)

                @pl.when(wanted)
                def _():
                    finish(way, to_chip, behind, part)

        if chips > 2:
            @pl.when(step == 0)
            def _():
                relay()

        @pl.when(step == own_step)
        def _():
            own_terms()

        return carry

    if chips == 2:
        relay()

    lax.fori_loop(0, chips - 1, step_body, 0)

    @pl.when(jnp.logical_not(has_near))
    def _():
        conv_ready()

    for part in range(2):
        add_conv(2, part, block, (0, 1))

    @pl.when(outer)
    def _():
        @pl.when(has_north)
        def _():
            far_south.wait_recv()

        @pl.when(has_south)
        def _():
            far_north.wait_recv()

        for part in range(2):
            add_conv(2, part, block, (2,))

    for part in range(2):
        for way, behind in enumerate((has_low, has_high)):
            @pl.when(behind)
            def _():
                line_copy(way, chip, part).wait_recv()
                acc[2, parts[part], :] += recv_buf[way, chip, parts[part], :].astype(F32)

        out[parts[part], :] = acc[2, parts[part], :]

    keep.wait()
    for copy in tile_copies:
        copy.wait_send()
    list_copy.wait_send()
    to_side.wait_send()

    @pl.when(outer)
    def _():
        around.wait_send()

        @pl.when(has_north)
        def _():
            far_north.wait_send()

        @pl.when(has_south)
        def _():
            far_south.wait_send()

    @pl.when(has_north)
    def _():
        to_north.wait_send()
        relays[0].wait_send()

    @pl.when(has_south)
    def _():
        to_south.wait_send()
        relays[1].wait_send()

    def drain(step, carry):
        for way in range(2):
            to_chip, wanted, _ = step_of(way, step)

            @pl.when(wanted)
            def _():
                for part in range(2):
                    line_copy(way, to_chip, part).wait_send()
        return carry

    lax.fori_loop(0, chips - 1, drain, 0)


def analyse_kernel(
    packed, state_mean, spread, out, anomaly_buf, out_buf, y, u, w, e, f, h, t, load, store
):
    members = spread.shape[0]
    fetch = pltpu.make_async_copy(spread, anomaly_buf, load)
    fetch.start()
    half, lane_blocks = members // 2, members // LANES
    blocks = [packed[at * half : (at + 1) * half] for at in range(lane_blocks)]
    cross = jnp.concatenate(blocks[: lane_blocks // 2], axis=1)
    field = jnp.concatenate(blocks[lane_blocks // 2 :], axis=1)
    tail = packed[lane_blocks * half :]

    def tail_row(first, count):
        at = [first * lane_blocks + each for each in range(count)]
        return jnp.concatenate(
            [tail[each : each + 1] + tail[each + lane_blocks : each + lane_blocks + 1] for each in at], axis=1
        )

    drive = tail_row(0, lane_blocks)
    diagonal = tail_row(2, lane_blocks // 2)
    row, col = iota((half, half), 0), iota((half, half), 1)
    on = row == col
    turned = field.T
    first = jnp.where(row < col, field, turned) + jnp.where(on, members - 1.0, 0.0)
    second = jnp.where(on, diagonal + (members - 1.0), jnp.where(row > col, field, turned))
    lone = diagonal + (members - 1.0)
    apart = jnp.where(on, 0.0, field)
    kept = field + (members - 1.0)
    squares = 2.0 * (apart * apart + cross * cross) + jnp.where(on, kept * kept, 0.0)
    square_sum = jnp.sum(
        jnp.sum(squares, axis=0, keepdims=True) + lone * lone, axis=1, keepdims=True
    )
    scale = jnp.sqrt(square_sum)
    shrink = 1.0 / scale
    upper_right = cross * shrink
    y[:half, :half] = (first * shrink).astype(BF16)
    y[half:, half:] = (second * shrink).astype(BF16)
    y[:half, half:] = upper_right.astype(BF16)
    y[half:, :half] = upper_right.T.astype(BF16)

    bands = [slice(at * half, (at + 1) * half) for at in range(2)]
    for band in bands:
        own = y[band, :].astype(F32)
        square = dot(y[band, :], y[...])
        u[band, :] = (1.5 * own - 0.5 * square).astype(BF16)
        w[band, :] = (0.25 * square - 1.5 * own).astype(BF16)
    for band in bands:
        product = dot(u[band, :], w[...])
        e[band, :] = (
            -0.75 * y[band, :].astype(F32) - 1.125 * u[band, :].astype(F32) - 0.5 * product
        ).astype(BF16)
    for band in bands:
        f[band, :] = (2.25 * y[band, :].astype(F32) + dot(y[band, :], e[...])).astype(BF16)
        h[band, :] = (4.5 * e[band, :].astype(F32) + dot(e[band, :], e[...])).astype(BF16)
    def times(vector, matrix):
        high = vector.astype(BF16)
        low = (vector - high.astype(F32)).astype(BF16)
        place = iota((16, members), 0)
        both = jnp.where(place == 0, high.astype(F32), jnp.where(place == 1, low.astype(F32), 0.0))
        product = dot(both.astype(BF16), matrix[...])
        return product[0:1] + product[1:2]

    drive_f = times(drive, f)
    push = 3.375 * drive + 1.5 * times(drive, e) - 2.53125 * drive_f - 0.5 * times(drive_f, h)
    for band in bands:
        product = dot(f[band, :], h[...])
        t[band, :] = (
            1.5 * e[band, :].astype(F32) - 2.53125 * f[band, :].astype(F32) - 0.5 * product
        ).astype(BF16)
    mean_weight = (3.375 * push + times(push, t)) * shrink
    gain = jnp.sqrt((members - 1.0) * shrink)
    fetch.wait()
    part = members // STORES
    stores = [
        pltpu.make_async_copy(
            out_buf.at[pl.ds(at * part, part)], out.at[0, 0, pl.ds(at * part, part)], store.at[at]
        )
        for at in range(STORES)
    ]
    for at, copy in enumerate(stores):
        band = slice(at * part, (at + 1) * part)
        one = iota((part, members), 0) + at * part == iota((part, members), 1)
        root = t[band, :].astype(F32) + jnp.where(one, 3.375, 0.0)
        transform = (gain * root + mean_weight).astype(BF16)
        out_buf[band, :] = dot(transform, anomaly_buf[...]) + state_mean[0:1]
        copy.start()
    for copy in stores:
        copy.wait()


def shards(
    n_lat, n_lon,
    background, conv_pert, conv_misfit, conv_column, sat_pert, sat_misfit, sat_rows, sat_targets,
):
    members, cells = background.shape[2:]
    tiles, tile_obs = sat_pert.shape[1:3]
    conv_obs = conv_pert.shape[2]
    rows, chips, half = tiles * tile_obs, n_lon // 2, members // 2
    vmem = pl.BlockSpec(memory_space=pltpu.VMEM)
    lanes_long = members // LANES * half + EXTRA
    hbm = pl.BlockSpec(memory_space=pltpu.HBM)
    packed, anomaly, state_mean = pl.pallas_call(
        functools.partial(gather_kernel, n_lat, n_lon),
        out_shape=(
            jax.ShapeDtypeStruct((lanes_long, LANES), F32),
            jax.ShapeDtypeStruct((members, cells), BF16),
            jax.ShapeDtypeStruct((8, cells), F32),
        ),
        in_specs=[hbm] * 8,
        out_specs=(vmem, hbm, vmem),
        scratch_shapes=[
            pltpu.VMEM((members, cells), BF16),
            pltpu.VMEM((members, cells), BF16),
            pltpu.VMEM((1, 1, conv_obs), BF16),
            pltpu.VMEM((1, 1, conv_obs), jnp.int32),
            pltpu.VMEM((1, tiles, tile_obs), BF16),
            pltpu.VMEM((1, tiles), jnp.int32),
            pltpu.VMEM((1, 2, tiles), jnp.int32),
            pltpu.VMEM((2, rows, members), BF16),
            pltpu.VMEM((2, EXTRA, rows), BF16),
            pltpu.VMEM((3, 3, conv_obs + EXTRA, members), BF16),
            pltpu.VMEM((2, members, rows), BF16),
            pltpu.VMEM((members, 6 * conv_obs), BF16),
            pltpu.VMEM((3, lanes_long, LANES), F32),
            pltpu.VMEM((2, chips, lanes_long, LANES), BF16),
            pltpu.VMEM((2, chips, lanes_long, LANES), BF16),
            pltpu.SemaphoreType.DMA((9,)),
            pltpu.SemaphoreType.DMA((3,)),
            pltpu.SemaphoreType.DMA((3,)),
            pltpu.SemaphoreType.DMA((8,)),
            pltpu.SemaphoreType.DMA((8,)),
            pltpu.SemaphoreType.DMA((2, chips, 2)),
            pltpu.SemaphoreType.DMA((2, chips, 2)),
        ],
        compiler_params=pltpu.CompilerParams(
            collective_id=0, has_side_effects=True, vmem_limit_bytes=64 * 1024 * 1024
        ),
        cost_estimate=pl.CostEstimate(
            flops=2 * (chips * 2 * rows + 9 * conv_obs) * members * members,
            bytes_accessed=4 * rows * members, transcendentals=0,
        ),
        name="gather_grams",
    )(
        background, conv_pert, conv_misfit, conv_column, sat_pert.reshape(rows, members), sat_misfit, sat_rows,
        jnp.swapaxes(sat_targets, 1, 2),
    )
    return pl.pallas_call(
        analyse_kernel,
        out_shape=jax.ShapeDtypeStruct((1, 1, members, cells), F32),
        in_specs=[vmem, vmem, hbm],
        out_specs=hbm,
        scratch_shapes=[
            pltpu.VMEM((members, cells), BF16),
            pltpu.VMEM((members, cells), F32),
            *[pltpu.VMEM((members, members), BF16)] * 7,
            pltpu.SemaphoreType.DMA,
            pltpu.SemaphoreType.DMA((STORES,)),
        ],
        compiler_params=pltpu.CompilerParams(vmem_limit_bytes=64 * 1024 * 1024),
        cost_estimate=pl.CostEstimate(
            flops=14 * members * members * members, bytes_accessed=6 * members * cells, transcendentals=0
        ),
        name="analyse",
    )(packed, state_mean, anomaly)


def solution(mesh):
    placed = (
        P("lat", "lon", None, None),
        P("lat", "lon", None, None),
        P("lat", "lon", None),
        P("lat", "lon", None),
        P("lat", "lon", None, None),
        P("lat", "lon", None),
        P("lat", "lon"),
        P("lat", "lon", None),
    )
    return jax.shard_map(
        functools.partial(shards, mesh.shape["lat"], mesh.shape["lon"]),
        mesh=mesh, in_specs=placed, out_specs=P("lat", "lon", None, None), check_vma=False,
    )
```

```python
import functools

import jax
import jax.numpy as jnp
from jax import lax
from jax.experimental import pallas as pl
from jax.experimental.pallas import tpu as pltpu
from jax.sharding import PartitionSpec as P

BLK = 16
MESH = pl.DeviceIdType.MESH
F32 = jnp.float32
BF16 = jnp.bfloat16
EXTRA = 16
LANES = 128
STORES = 2


def dot(left, right):
    return lax.dot_general(left, right, (((1,), (0,)), ((), ())), preferred_element_type=F32)


def iota(shape, dim):
    return lax.broadcasted_iota(jnp.int32, shape, dim)


def gather_kernel(
    n_lat, n_lon,
    background, conv_pert, conv_misfit, conv_column, sat_pert, sat_misfit, sat_rows, sat_targets,
    out, anomaly, centre,
    members_buf, anomaly_buf, small_misfit, small_column, tile_misfit, tile_rows, tile_targets,
    sat_buf, sat_lists, conv_buf, sat_flip, conv_flip, acc, send_buf, recv_buf,
    load, sat_send, sat_recv, conv_send, conv_recv, line_send, line_recv,
):
    chips = n_lon // 2
    band = lax.axis_index("lat")
    block = lax.axis_index("lon")
    chip, core = block // 2, block % 2
    sibling = 2 * chip + (1 - core)
    opposite = n_lon - 1 - block
    tiles, tile_obs = sat_misfit.shape[1], sat_misfit.shape[2]
    rows, members = tiles * tile_obs, sat_pert.shape[1]
    conv_obs = conv_pert.shape[2]
    half, lane_blocks = members // 2, members // LANES
    has_north, has_south = band > 0, band < n_lat - 1
    has_low, has_high = chip > 0, chip < chips - 1
    outer = jnp.logical_or(block == 0, block == n_lon - 1)
    mates = (
        (has_north, (band - 1, block)),
        (has_south, (band + 1, block)),
        (has_low, (band, block - 2)),
        (has_high, (band, block + 2)),
        (outer, (band, opposite)),
    )

    barrier = pltpu.get_barrier_semaphore()
    pl.semaphore_signal(barrier, inc=1, device_id=(band, sibling), device_id_type=MESH)
    for here, mate in mates:
        @pl.when(here)
        def _():
            pl.semaphore_signal(barrier, inc=1, device_id=mate, device_id_type=MESH)

    loads = [
        pltpu.make_async_copy(source, target, load.at[at])
        for at, (source, target) in enumerate(
            (
                (conv_pert.at[0, 0], conv_buf.at[0, 1, pl.ds(0, conv_obs)]),
                (conv_misfit, small_misfit),
                (conv_column, small_column),
                (sat_misfit, tile_misfit),
                (sat_rows, tile_rows),
                (sat_targets, tile_targets),
                (sat_pert, sat_buf.at[0]),
                (background.at[0, 0], members_buf),
            )
        )
    ]
    for copy in loads:
        copy.start()
    pl.semaphore_wait(barrier, 1 + sum(here.astype(jnp.int32) for here, _ in mates))

    def sat_copy(source, target, at):
        return pltpu.make_async_remote_copy(
            src_ref=source, dst_ref=target, send_sem=sat_send.at[at], recv_sem=sat_recv.at[at],
            device_id=(band, sibling), device_id_type=MESH,
        )

    spans = [pl.ds(at * (rows // 2), rows // 2) for at in range(2)]
    tile_copies = [sat_copy(sat_pert.at[span], sat_buf.at[1, span], at) for at, span in enumerate(spans)]
    list_copy = sat_copy(sat_lists.at[0], sat_lists.at[1], 2)
    for copy in tile_copies:
        copy.start()

    for copy in loads[:6]:
        copy.wait()
    conv_buf[0, 1, conv_obs:, :] = jnp.concatenate(
        [
            jnp.broadcast_to(small_column[0].astype(F32).astype(BF16), (EXTRA, conv_obs)),
            jnp.broadcast_to(small_misfit[0], (EXTRA, conv_obs)),
            jnp.zeros((EXTRA, members - 2 * conv_obs), BF16),
        ],
        axis=1,
    )

    def conv_copy(group, slot, to_group, to_slot, sem, mate):
        return pltpu.make_async_remote_copy(
            src_ref=conv_buf.at[group, slot], dst_ref=conv_buf.at[to_group, to_slot],
            send_sem=conv_send.at[sem], recv_sem=conv_recv.at[sem],
            device_id=mate, device_id_type=MESH,
        )

    to_north = conv_copy(0, 1, 0, 2, 0, (band - 1, block))
    to_south = conv_copy(0, 1, 0, 0, 1, (band + 1, block))
    to_side = conv_copy(0, 1, 1, 1, 2, (band, sibling))
    relays = [conv_copy(0, 0, 1, 0, 3, (band, sibling)), conv_copy(0, 2, 1, 2, 4, (band, sibling))]
    around = conv_copy(0, 1, 2, 1, 5, (band, opposite))
    far_north = conv_copy(2, 1, 2, 2, 6, (band - 1, block))
    far_south = conv_copy(2, 1, 2, 0, 7, (band + 1, block))

    @pl.when(outer)
    def _():
        around.start()

    @pl.when(has_north)
    def _():
        to_north.start()

    @pl.when(has_south)
    def _():
        to_south.start()

    own_tile = iota((tiles, rows), 1) // tile_obs == iota((tiles, rows), 0)
    own_mask = own_tile.astype(BF16)
    spread_obs = (iota((tile_obs, rows), 1) % tile_obs == iota((tile_obs, rows), 0)).astype(BF16)
    misfit = jnp.sum(jnp.where(own_tile, dot(tile_misfit[0], spread_obs), 0.0), axis=0, keepdims=True)
    count = dot(jnp.broadcast_to(tile_rows[...].astype(F32).astype(BF16), (8, tiles)), own_mask)[0:1]
    live = (iota((1, rows), 1) % tile_obs).astype(F32) < count
    names = tile_targets[0].astype(F32)
    lists = [
        jnp.where(
            live,
            dot(jnp.broadcast_to(names[e : e + 1], (8, tiles)).astype(BF16), own_mask)[0:1],
            -1.0,
        )
        for e in range(2)
    ]
    place = iota((EXTRA, rows), 0)
    sat_lists[0] = jnp.where(
        place == 0, lists[0], jnp.where(place == 1, lists[1], jnp.where(place == 2, misfit, 0.0))
    ).astype(BF16)
    list_copy.start()
    to_side.start()

    def flip_sat(side, part, span):
        lanes = slice(part * half, (part + 1) * half)
        sat_flip[side, lanes, span] = sat_buf[side, span, lanes].T

    def relay():
        blank = jnp.zeros((conv_obs + EXTRA, members), BF16)

        @pl.when(jnp.logical_not(has_north))
        def _():
            for group in range(3):
                conv_buf[group, 0] = blank

        @pl.when(jnp.logical_not(has_south))
        def _():
            for group in range(3):
                conv_buf[group, 2] = blank

        @pl.when(has_north)
        def _():
            to_south.wait_recv()
            relays[0].start()

        @pl.when(has_south)
        def _():
            to_north.wait_recv()
            relays[1].start()

        @pl.when(outer)
        def _():
            around.wait_recv()

            @pl.when(has_north)
            def _():
                far_north.start()

            @pl.when(has_south)
            def _():
                far_south.start()

    def conv_ready():
        to_side.wait_recv()

        @pl.when(has_north)
        def _():
            relays[0].wait_recv()

        @pl.when(has_south)
        def _():
            relays[1].wait_recv()

        for group in range(2):
            for slot in range(3):
                at = (group * 3 + slot) * conv_obs
                conv_flip[:, at : at + conv_obs] = conv_buf[group, slot, :conv_obs, :].T

    def conv_weight(group, slot, target):
        column = conv_buf[group, slot, conv_obs:, :conv_obs][0:1].astype(F32)
        source = (block, sibling, opposite)[group]
        away = lax.rem(source - target + 1 + n_lon, n_lon) - 1
        row = jnp.floor(column * (1.0 / BLK))
        lat_place = BLK * (slot - 1.0) + row + 0.5 - 0.5 * BLK
        lon_place = BLK * away.astype(F32) + (column - BLK * row) + 0.5 - 0.5 * BLK
        weight = jnp.exp(-(lat_place * lat_place + lon_place * lon_place) / (2.0 * BLK * BLK))
        return jnp.where(away <= 1, weight, 0.0)

    place = iota((EXTRA, LANES), 0)
    eye = iota((half, half), 0) == iota((half, half), 1)
    upper = iota((half, half), 0) <= iota((half, half), 1)

    cut = lane_blocks // 2 * half
    parts = (slice(0, cut), slice(cut, 2 * cut + EXTRA))

    def add_terms(slot, part, flipped, weight, push, spread, first):
        def put(into, term):
            if first:
                acc[slot, into, :] = term
            else:
                acc[slot, into, :] += term

        def scaled(rows_of):
            if weight.dtype == BF16:
                return rows_of * weight
            return (rows_of.astype(F32) * weight).astype(BF16)

        if part == 0:
            piece = dot(scaled(flipped[:half]), spread[:, half:])
        else:
            low = dot(scaled(flipped[half:]), spread[:, half:])
            piece = jnp.where(upper, dot(scaled(flipped[:half]), spread[:, :half]), low)
            drive = dot(jnp.broadcast_to(push, (EXTRA, push.shape[1])).astype(BF16), spread)
            diagonal = jnp.sum(jnp.where(eye, low, 0.0), axis=0, keepdims=True)
            tail = jnp.zeros((EXTRA, LANES), F32)
            for at in range(lane_blocks):
                lanes = slice(at * LANES, (at + 1) * LANES)
                tail += jnp.where(place == at, drive[0:1, lanes], 0.0)
                if at < lane_blocks // 2:
                    tail += jnp.where(place == 2 * lane_blocks + at, diagonal[:, lanes], 0.0)
            put(slice(2 * cut, 2 * cut + EXTRA), tail)
        for at in range(lane_blocks // 2):
            put(slice(part * cut + at * half, part * cut + (at + 1) * half), piece[:, at * LANES : (at + 1) * LANES])

    def add_conv(slot, part, target, groups):
        weights, pushes = [], []
        for group in groups:
            for side in range(3):
                weight = conv_weight(group, side, target)
                misfit = conv_buf[group, side, conv_obs:, conv_obs : 2 * conv_obs][0:1].astype(F32)
                weights.append(weight)
                pushes.append(weight * misfit)
        spreads = [conv_buf[group, side, :conv_obs, :] for group in groups for side in range(3)]
        flipped = conv_flip[...] if len(groups) == 2 else jnp.concatenate([each.T for each in spreads], axis=1)
        weight, push = (jnp.concatenate(each, axis=1) for each in (weights, pushes))
        add_terms(slot, part, flipped, weight, push, jnp.concatenate(spreads, axis=0), False)

    def add_sat(slot, part, to_chip, side):
        name = (2 * to_chip + core).astype(F32)
        lists = sat_lists[side].astype(F32)
        weight = jnp.where(lists[0:1] == name, 1.0, 0.0) + jnp.where(lists[1:2] == name, 0.5, 0.0)
        add_terms(
            slot, part, sat_flip[side], weight.astype(BF16), weight * lists[2:3], sat_buf[side], side == 0
        )

    has_near = jnp.where(core == 0, chip < chips - 1, chip > 0)
    near = chip + 1 - 2 * core

    def line_copy(way, to_chip, part):
        ahead = block + 2 if way == 0 else block - 2
        span = pl.ds(parts[part].start, parts[part].stop - parts[part].start)
        return pltpu.make_async_remote_copy(
            src_ref=send_buf.at[way, to_chip, span], dst_ref=recv_buf.at[way, to_chip, span],
            send_sem=line_send.at[way, to_chip, part], recv_sem=line_recv.at[way, to_chip, part],
            device_id=(band, ahead), device_id_type=MESH,
        )

    def step_of(way, step):
        if way == 0:
            to_chip = chips - 1 + chip - step
            return to_chip, jnp.logical_and(to_chip > chip, to_chip < chips), has_low
        to_chip = step + chip - chips + 1
        return to_chip, jnp.logical_and(to_chip >= 0, to_chip < chip), has_high

    def finish(way, to_chip, behind, part):
        @pl.when(behind)
        def _():
            line_copy(way, to_chip, part).wait_recv()
            acc[way, parts[part], :] += recv_buf[way, to_chip, parts[part], :].astype(F32)

        send_buf[way, to_chip, part * cut : (part + 1) * cut, :] = acc[
            way, part * cut : (part + 1) * cut, :
        ].astype(BF16)
        if part == 1:
            tail = acc[way, 2 * cut :, :]
            four = [tail[at * lane_blocks : (at + 1) * lane_blocks] for at in range(4)]
            high, kept = (four[at].astype(BF16).astype(F32) for at in (0, 2))
            send_buf[way, to_chip, 2 * cut :, :] = jnp.concatenate(
                [high, four[0] + four[1] - high, kept, four[2] + four[3] - kept], axis=0
            ).astype(BF16)
        line_copy(way, to_chip, part).start()

    loads[6].wait()
    for span in spans:
        flip_sat(0, 0, span)
    for way in range(2):
        to_chip, wanted, _ = step_of(way, 0)

        @pl.when(wanted)
        def _():
            add_sat(way, 0, to_chip, 0)

    list_copy.wait_recv()
    for copy, span in zip(tile_copies, spans):
        copy.wait_recv()
        flip_sat(1, 0, span)

    keep = pltpu.make_async_copy(anomaly_buf, anomaly, load.at[8])

    own_step = jnp.where(jnp.logical_and(has_low, has_high), 0, chips - 2)

    def own_terms():
        for part in range(2):
            for side in range(2):
                add_sat(2, part, chip, side)
        loads[7].wait()
        ensemble = members_buf[...].astype(F32)
        state_mean = jnp.mean(ensemble, axis=0, keepdims=True)
        anomaly_buf[...] = (ensemble - state_mean).astype(BF16)
        keep.start()
        centre[...] = jnp.broadcast_to(state_mean, centre.shape)

    def step_body(step, carry):
        for part in range(2):
            if part == 1:
                @pl.when(step == 0)
                def _():
                    for side in range(2):
                        for span in spans:
                            flip_sat(side, 1, span)

            for way in range(2):
                to_chip, wanted, behind = step_of(way, step)

                @pl.when(wanted)
                def _():
                    @pl.when(jnp.logical_or(step > 0, part == 1))
                    def _():
                        add_sat(way, part, to_chip, 0)

                    add_sat(way, part, to_chip, 1)

                    @pl.when(to_chip == near)
                    def _():
                        if part == 0:
                            conv_ready()
                        add_conv(way, part, 2 * to_chip + core, (0, 1))

            for way in range(2):
                to_chip, wanted, behind = step_of(way, step)

                @pl.when(wanted)
                def _():
                    finish(way, to_chip, behind, part)

        @pl.when(step == own_step)
        def _():
            own_terms()

        if chips > 2:
            @pl.when(step == chips - 3)
            def _():
                relay()

        return carry

    if chips == 2:
        relay()

    lax.fori_loop(0, chips - 1, step_body, 0)

    @pl.when(jnp.logical_not(has_near))
    def _():
        conv_ready()

    for part in range(2):
        add_conv(2, part, block, (0, 1))

    @pl.when(outer)
    def _():
        @pl.when(has_north)
        def _():
            far_south.wait_recv()

        @pl.when(has_south)
        def _():
            far_north.wait_recv()

        for part in range(2):
            add_conv(2, part, block, (2,))

    for part in range(2):
        for way, behind in enumerate((has_low, has_high)):
            @pl.when(behind)
            def _():
                line_copy(way, chip, part).wait_recv()
                acc[2, parts[part], :] += recv_buf[way, chip, parts[part], :].astype(F32)

        out[parts[part], :] = acc[2, parts[part], :]

    keep.wait()
    for copy in tile_copies:
        copy.wait_send()
    list_copy.wait_send()
    to_side.wait_send()

    @pl.when(outer)
    def _():
        around.wait_send()

        @pl.when(has_north)
        def _():
            far_north.wait_send()

        @pl.when(has_south)
        def _():
            far_south.wait_send()

    @pl.when(has_north)
    def _():
        to_north.wait_send()
        relays[0].wait_send()

    @pl.when(has_south)
    def _():
        to_south.wait_send()
        relays[1].wait_send()

    def drain(step, carry):
        for way in range(2):
            to_chip, wanted, _ = step_of(way, step)

            @pl.when(wanted)
            def _():
                for part in range(2):
                    line_copy(way, to_chip, part).wait_send()
        return carry

    lax.fori_loop(0, chips - 1, drain, 0)


def analyse_kernel(
    packed, state_mean, spread, out, anomaly_buf, out_buf, y, u, w, e, f, h, t, load, store
):
    members = spread.shape[0]
    fetch = pltpu.make_async_copy(spread, anomaly_buf, load)
    fetch.start()
    half, lane_blocks = members // 2, members // LANES
    blocks = [packed[at * half : (at + 1) * half] for at in range(lane_blocks)]
    cross = jnp.concatenate(blocks[: lane_blocks // 2], axis=1)
    field = jnp.concatenate(blocks[lane_blocks // 2 :], axis=1)
    tail = packed[lane_blocks * half :]

    def tail_row(first, count):
        at = [first * lane_blocks + each for each in range(count)]
        return jnp.concatenate(
            [tail[each : each + 1] + tail[each + lane_blocks : each + lane_blocks + 1] for each in at], axis=1
        )

    drive = tail_row(0, lane_blocks)
    diagonal = tail_row(2, lane_blocks // 2)
    row, col = iota((half, half), 0), iota((half, half), 1)
    on = row == col
    turned = field.T
    first = jnp.where(row < col, field, turned) + jnp.where(on, members - 1.0, 0.0)
    second = jnp.where(on, diagonal + (members - 1.0), jnp.where(row > col, field, turned))
    lone = diagonal + (members - 1.0)
    apart = jnp.where(on, 0.0, field)
    kept = field + (members - 1.0)
    squares = 2.0 * (apart * apart + cross * cross) + jnp.where(on, kept * kept, 0.0)
    square_sum = jnp.sum(
        jnp.sum(squares, axis=0, keepdims=True) + lone * lone, axis=1, keepdims=True
    )
    scale = jnp.sqrt(square_sum)
    shrink = 1.0 / scale
    upper_right = cross * shrink
    y[:half, :half] = (first * shrink).astype(BF16)
    y[half:, half:] = (second * shrink).astype(BF16)
    y[:half, half:] = upper_right.astype(BF16)
    y[half:, :half] = upper_right.T.astype(BF16)

    bands = [slice(0, members)]
    for band in bands:
        own = y[band, :].astype(F32)
        square = dot(y[band, :], y[...])
        u[band, :] = (1.5 * own - 0.5 * square).astype(BF16)
        w[band, :] = (0.25 * square - 1.5 * own).astype(BF16)
    for band in bands:
        product = dot(u[band, :], w[...])
        e[band, :] = (
            -0.75 * y[band, :].astype(F32) - 1.125 * u[band, :].astype(F32) - 0.5 * product
        ).astype(BF16)
    for band in bands:
        f[band, :] = (2.25 * y[band, :].astype(F32) + dot(y[band, :], e[...])).astype(BF16)
        h[band, :] = (4.5 * e[band, :].astype(F32) + dot(e[band, :], e[...])).astype(BF16)
    def times(vector, matrix):
        high = vector.astype(BF16)
        low = (vector - high.astype(F32)).astype(BF16)
        place = iota((16, members), 0)
        both = jnp.where(place == 0, high.astype(F32), jnp.where(place == 1, low.astype(F32), 0.0))
        product = dot(both.astype(BF16), matrix[...])
        return product[0:1] + product[1:2]

    drive_f = times(drive, f)
    push = 3.375 * drive + 1.5 * times(drive, e) - 2.53125 * drive_f - 0.5 * times(drive_f, h)
    for band in bands:
        product = dot(f[band, :], h[...])
        t[band, :] = (
            1.5 * e[band, :].astype(F32) - 2.53125 * f[band, :].astype(F32) - 0.5 * product
        ).astype(BF16)
    mean_weight = (3.375 * push + times(push, t)) * shrink
    gain = jnp.sqrt((members - 1.0) * shrink)
    fetch.wait()
    part = members // STORES
    stores = [
        pltpu.make_async_copy(
            out_buf.at[pl.ds(at * part, part)], out.at[0, 0, pl.ds(at * part, part)], store.at[at]
        )
        for at in range(STORES)
    ]
    for at, copy in enumerate(stores):
        band = slice(at * part, (at + 1) * part)
        one = iota((part, members), 0) + at * part == iota((part, members), 1)
        root = t[band, :].astype(F32) + jnp.where(one, 3.375, 0.0)
        transform = (gain * root + mean_weight).astype(BF16)
        out_buf[band, :] = dot(transform, anomaly_buf[...]) + state_mean[0:1]
        copy.start()
    for copy in stores:
        copy.wait()


def shards(
    n_lat, n_lon,
    background, conv_pert, conv_misfit, conv_column, sat_pert, sat_misfit, sat_rows, sat_targets,
):
    members, cells = background.shape[2:]
    tiles, tile_obs = sat_pert.shape[1:3]
    conv_obs = conv_pert.shape[2]
    rows, chips, half = tiles * tile_obs, n_lon // 2, members // 2
    vmem = pl.BlockSpec(memory_space=pltpu.VMEM)
    lanes_long = members // LANES * half + EXTRA
    hbm = pl.BlockSpec(memory_space=pltpu.HBM)
    packed, anomaly, state_mean = pl.pallas_call(
        functools.partial(gather_kernel, n_lat, n_lon),
        out_shape=(
            jax.ShapeDtypeStruct((lanes_long, LANES), F32),
            jax.ShapeDtypeStruct((members, cells), BF16),
            jax.ShapeDtypeStruct((8, cells), F32),
        ),
        in_specs=[hbm] * 8,
        out_specs=(vmem, hbm, vmem),
        scratch_shapes=[
            pltpu.VMEM((members, cells), BF16),
            pltpu.VMEM((members, cells), BF16),
            pltpu.VMEM((1, 1, conv_obs), BF16),
            pltpu.VMEM((1, 1, conv_obs), jnp.int32),
            pltpu.VMEM((1, tiles, tile_obs), BF16),
            pltpu.VMEM((1, tiles), jnp.int32),
            pltpu.VMEM((1, 2, tiles), jnp.int32),
            pltpu.VMEM((2, rows, members), BF16),
            pltpu.VMEM((2, EXTRA, rows), BF16),
            pltpu.VMEM((3, 3, conv_obs + EXTRA, members), BF16),
            pltpu.VMEM((2, members, rows), BF16),
            pltpu.VMEM((members, 6 * conv_obs), BF16),
            pltpu.VMEM((3, lanes_long, LANES), F32),
            pltpu.VMEM((2, chips, lanes_long, LANES), BF16),
            pltpu.VMEM((2, chips, lanes_long, LANES), BF16),
            pltpu.SemaphoreType.DMA((9,)),
            pltpu.SemaphoreType.DMA((3,)),
            pltpu.SemaphoreType.DMA((3,)),
            pltpu.SemaphoreType.DMA((8,)),
            pltpu.SemaphoreType.DMA((8,)),
            pltpu.SemaphoreType.DMA((2, chips, 2)),
            pltpu.SemaphoreType.DMA((2, chips, 2)),
        ],
        compiler_params=pltpu.CompilerParams(
            collective_id=0, has_side_effects=True, vmem_limit_bytes=64 * 1024 * 1024
        ),
        cost_estimate=pl.CostEstimate(
            flops=2 * (chips * 2 * rows + 9 * conv_obs) * members * members,
            bytes_accessed=4 * rows * members, transcendentals=0,
        ),
        name="gather_grams",
    )(
        background, conv_pert, conv_misfit, conv_column, sat_pert.reshape(rows, members), sat_misfit, sat_rows,
        jnp.swapaxes(sat_targets, 1, 2),
    )
    return pl.pallas_call(
        analyse_kernel,
        out_shape=jax.ShapeDtypeStruct((1, 1, members, cells), F32),
        in_specs=[vmem, vmem, hbm],
        out_specs=hbm,
        scratch_shapes=[
            pltpu.VMEM((members, cells), BF16),
            pltpu.VMEM((members, cells), F32),
            *[pltpu.VMEM((members, members), BF16)] * 7,
            pltpu.SemaphoreType.DMA,
            pltpu.SemaphoreType.DMA((STORES,)),
        ],
        compiler_params=pltpu.CompilerParams(vmem_limit_bytes=64 * 1024 * 1024),
        cost_estimate=pl.CostEstimate(
            flops=14 * members * members * members, bytes_accessed=6 * members * cells, transcendentals=0
        ),
        name="analyse",
    )(packed, state_mean, anomaly)


def solution(mesh):
    placed = (
        P("lat", "lon", None, None),
        P("lat", "lon", None, None),
        P("lat", "lon", None),
        P("lat", "lon", None),
        P("lat", "lon", None, None),
        P("lat", "lon", None),
        P("lat", "lon"),
        P("lat", "lon", None),
    )
    return jax.shard_map(
        functools.partial(shards, mesh.shape["lat"], mesh.shape["lon"]),
        mesh=mesh, in_specs=placed, out_specs=P("lat", "lon", None, None), check_vma=False,
    )
```

```python
import functools

import jax
import jax.numpy as jnp
from jax import lax
from jax.experimental import pallas as pl
from jax.experimental.pallas import tpu as pltpu
from jax.sharding import PartitionSpec as P

BLK = 16
MESH = pl.DeviceIdType.MESH
F32 = jnp.float32
BF16 = jnp.bfloat16
EXTRA = 16
LANES = 128
STORES = 4


def dot(left, right):
    return lax.dot_general(left, right, (((1,), (0,)), ((), ())), preferred_element_type=F32)


def iota(shape, dim):
    return lax.broadcasted_iota(jnp.int32, shape, dim)


def gather_kernel(
    n_lat, n_lon,
    background, conv_pert, conv_misfit, conv_column, sat_pert, sat_misfit, sat_rows, sat_targets,
    out, anomaly, centre,
    members_buf, anomaly_buf, small_misfit, small_column, tile_misfit, tile_rows, tile_targets,
    sat_buf, sat_lists, conv_buf, sat_flip, conv_flip, acc, send_buf, recv_buf,
    load, sat_send, sat_recv, conv_send, conv_recv, line_send, line_recv,
):
    chips = n_lon // 2
    band = lax.axis_index("lat")
    block = lax.axis_index("lon")
    chip, core = block // 2, block % 2
    sibling = 2 * chip + (1 - core)
    opposite = n_lon - 1 - block
    tiles, tile_obs = sat_misfit.shape[1], sat_misfit.shape[2]
    rows, members = tiles * tile_obs, sat_pert.shape[1]
    conv_obs = conv_pert.shape[2]
    half, lane_blocks = members // 2, members // LANES
    has_north, has_south = band > 0, band < n_lat - 1
    has_low, has_high = chip > 0, chip < chips - 1
    outer = jnp.logical_or(block == 0, block == n_lon - 1)
    mates = (
        (has_north, (band - 1, block)),
        (has_south, (band + 1, block)),
        (has_low, (band, block - 2)),
        (has_high, (band, block + 2)),
        (outer, (band, opposite)),
    )

    barrier = pltpu.get_barrier_semaphore()
    pl.semaphore_signal(barrier, inc=1, device_id=(band, sibling), device_id_type=MESH)
    for here, mate in mates:
        @pl.when(here)
        def _():
            pl.semaphore_signal(barrier, inc=1, device_id=mate, device_id_type=MESH)

    loads = [
        pltpu.make_async_copy(source, target, load.at[at])
        for at, (source, target) in enumerate(
            (
                (conv_pert.at[0, 0], conv_buf.at[0, 1, pl.ds(0, conv_obs)]),
                (conv_misfit, small_misfit),
                (conv_column, small_column),
                (sat_misfit, tile_misfit),
                (sat_rows, tile_rows),
                (sat_targets, tile_targets),
                (sat_pert, sat_buf.at[0]),
                (background.at[0, 0], members_buf),
            )
        )
    ]
    for copy in loads:
        copy.start()
    pl.semaphore_wait(barrier, 1 + sum(here.astype(jnp.int32) for here, _ in mates))

    def sat_copy(source, target, at):
        return pltpu.make_async_remote_copy(
            src_ref=source, dst_ref=target, send_sem=sat_send.at[at], recv_sem=sat_recv.at[at],
            device_id=(band, sibling), device_id_type=MESH,
        )

    spans = [pl.ds(at * (rows // 2), rows // 2) for at in range(2)]
    tile_copies = [sat_copy(sat_pert.at[span], sat_buf.at[1, span], at) for at, span in enumerate(spans)]
    list_copy = sat_copy(sat_lists.at[0], sat_lists.at[1], 2)
    for copy in tile_copies:
        copy.start()

    for copy in loads[:6]:
        copy.wait()
    conv_buf[0, 1, conv_obs:, :] = jnp.concatenate(
        [
            jnp.broadcast_to(small_column[0].astype(F32).astype(BF16), (EXTRA, conv_obs)),
            jnp.broadcast_to(small_misfit[0], (EXTRA, conv_obs)),
            jnp.zeros((EXTRA, members - 2 * conv_obs), BF16),
        ],
        axis=1,
    )

    def conv_copy(group, slot, to_group, to_slot, sem, mate):
        return pltpu.make_async_remote_copy(
            src_ref=conv_buf.at[group, slot], dst_ref=conv_buf.at[to_group, to_slot],
            send_sem=conv_send.at[sem], recv_sem=conv_recv.at[sem],
            device_id=mate, device_id_type=MESH,
        )

    to_north = conv_copy(0, 1, 0, 2, 0, (band - 1, block))
    to_south = conv_copy(0, 1, 0, 0, 1, (band + 1, block))
    to_side = conv_copy(0, 1, 1, 1, 2, (band, sibling))
    relays = [conv_copy(0, 0, 1, 0, 3, (band, sibling)), conv_copy(0, 2, 1, 2, 4, (band, sibling))]
    around = conv_copy(0, 1, 2, 1, 5, (band, opposite))
    far_north = conv_copy(2, 1, 2, 2, 6, (band - 1, block))
    far_south = conv_copy(2, 1, 2, 0, 7, (band + 1, block))

    @pl.when(outer)
    def _():
        around.start()

    @pl.when(has_north)
    def _():
        to_north.start()

    @pl.when(has_south)
    def _():
        to_south.start()

    own_tile = iota((tiles, rows), 1) // tile_obs == iota((tiles, rows), 0)
    own_mask = own_tile.astype(BF16)
    spread_obs = (iota((tile_obs, rows), 1) % tile_obs == iota((tile_obs, rows), 0)).astype(BF16)
    misfit = jnp.sum(jnp.where(own_tile, dot(tile_misfit[0], spread_obs), 0.0), axis=0, keepdims=True)
    count = dot(jnp.broadcast_to(tile_rows[...].astype(F32).astype(BF16), (8, tiles)), own_mask)[0:1]
    live = (iota((1, rows), 1) % tile_obs).astype(F32) < count
    names = tile_targets[0].astype(F32)
    lists = [
        jnp.where(
            live,
            dot(jnp.broadcast_to(names[e : e + 1], (8, tiles)).astype(BF16), own_mask)[0:1],
            -1.0,
        )
        for e in range(2)
    ]
    place = iota((EXTRA, rows), 0)
    sat_lists[0] = jnp.where(
        place == 0, lists[0], jnp.where(place == 1, lists[1], jnp.where(place == 2, misfit, 0.0))
    ).astype(BF16)
    list_copy.start()
    to_side.start()

    def flip_sat(side, part, span):
        lanes = slice(part * half, (part + 1) * half)
        sat_flip[side, lanes, span] = sat_buf[side, span, lanes].T

    def relay():
        blank = jnp.zeros((conv_obs + EXTRA, members), BF16)

        @pl.when(jnp.logical_not(has_north))
        def _():
            for group in range(3):
                conv_buf[group, 0] = blank

        @pl.when(jnp.logical_not(has_south))
        def _():
            for group in range(3):
                conv_buf[group, 2] = blank

        @pl.when(has_north)
        def _():
            to_south.wait_recv()
            relays[0].start()

        @pl.when(has_south)
        def _():
            to_north.wait_recv()
            relays[1].start()

        @pl.when(outer)
        def _():
            around.wait_recv()

            @pl.when(has_north)
            def _():
                far_north.start()

            @pl.when(has_south)
            def _():
                far_south.start()

    def conv_ready():
        to_side.wait_recv()

        @pl.when(has_north)
        def _():
            relays[0].wait_recv()

        @pl.when(has_south)
        def _():
            relays[1].wait_recv()

        for group in range(2):
            for slot in range(3):
                at = (group * 3 + slot) * conv_obs
                conv_flip[:, at : at + conv_obs] = conv_buf[group, slot, :conv_obs, :].T

    def conv_weight(group, slot, target):
        column = conv_buf[group, slot, conv_obs:, :conv_obs][0:1].astype(F32)
        source = (block, sibling, opposite)[group]
        away = lax.rem(source - target + 1 + n_lon, n_lon) - 1
        row = jnp.floor(column * (1.0 / BLK))
        lat_place = BLK * (slot - 1.0) + row + 0.5 - 0.5 * BLK
        lon_place = BLK * away.astype(F32) + (column - BLK * row) + 0.5 - 0.5 * BLK
        weight = jnp.exp(-(lat_place * lat_place + lon_place * lon_place) / (2.0 * BLK * BLK))
        return jnp.where(away <= 1, weight, 0.0)

    place = iota((EXTRA, LANES), 0)
    eye = iota((half, half), 0) == iota((half, half), 1)
    upper = iota((half, half), 0) <= iota((half, half), 1)

    cut = lane_blocks // 2 * half
    parts = (slice(0, cut), slice(cut, 2 * cut + EXTRA))

    def add_terms(slot, part, flipped, weight, push, spread, first):
        def put(into, term):
            if first:
                acc[slot, into, :] = term
            else:
                acc[slot, into, :] += term

        def scaled(rows_of):
            if weight.dtype == BF16:
                return rows_of * weight
            return (rows_of.astype(F32) * weight).astype(BF16)

        if part == 0:
            piece = dot(scaled(flipped[:half]), spread[:, half:])
        else:
            low = dot(scaled(flipped[half:]), spread[:, half:])
            piece = jnp.where(upper, dot(scaled(flipped[:half]), spread[:, :half]), low)
            drive = dot(jnp.broadcast_to(push, (EXTRA, push.shape[1])).astype(BF16), spread)
            diagonal = jnp.sum(jnp.where(eye, low, 0.0), axis=0, keepdims=True)
            tail = jnp.zeros((EXTRA, LANES), F32)
            for at in range(lane_blocks):
                lanes = slice(at * LANES, (at + 1) * LANES)
                tail += jnp.where(place == at, drive[0:1, lanes], 0.0)
                if at < lane_blocks // 2:
                    tail += jnp.where(place == 2 * lane_blocks + at, diagonal[:, lanes], 0.0)
            put(slice(2 * cut, 2 * cut + EXTRA), tail)
        for at in range(lane_blocks // 2):
            put(slice(part * cut + at * half, part * cut + (at + 1) * half), piece[:, at * LANES : (at + 1) * LANES])

    def add_conv(slot, part, target, groups):
        weights, pushes = [], []
        for group in groups:
            for side in range(3):
                weight = conv_weight(group, side, target)
                misfit = conv_buf[group, side, conv_obs:, conv_obs : 2 * conv_obs][0:1].astype(F32)
                weights.append(weight)
                pushes.append(weight * misfit)
        spreads = [conv_buf[group, side, :conv_obs, :] for group in groups for side in range(3)]
        flipped = conv_flip[...] if len(groups) == 2 else jnp.concatenate([each.T for each in spreads], axis=1)
        weight, push = (jnp.concatenate(each, axis=1) for each in (weights, pushes))
        add_terms(slot, part, flipped, weight, push, jnp.concatenate(spreads, axis=0), False)

    def add_sat(slot, part, to_chip, side):
        name = (2 * to_chip + core).astype(F32)
        lists = sat_lists[side].astype(F32)
        weight = jnp.where(lists[0:1] == name, 1.0, 0.0) + jnp.where(lists[1:2] == name, 0.5, 0.0)
        add_terms(
            slot, part, sat_flip[side], weight.astype(BF16), weight * lists[2:3], sat_buf[side], side == 0
        )

    has_near = jnp.where(core == 0, chip < chips - 1, chip > 0)
    near = chip + 1 - 2 * core

    def line_copy(way, to_chip, part):
        ahead = block + 2 if way == 0 else block - 2
        span = pl.ds(parts[part].start, parts[part].stop - parts[part].start)
        return pltpu.make_async_remote_copy(
            src_ref=send_buf.at[way, to_chip, span], dst_ref=recv_buf.at[way, to_chip, span],
            send_sem=line_send.at[way, to_chip, part], recv_sem=line_recv.at[way, to_chip, part],
            device_id=(band, ahead), device_id_type=MESH,
        )

    def step_of(way, step):
        if way == 0:
            to_chip = chips - 1 + chip - step
            return to_chip, jnp.logical_and(to_chip > chip, to_chip < chips), has_low
        to_chip = step + chip - chips + 1
        return to_chip, jnp.logical_and(to_chip >= 0, to_chip < chip), has_high

    def finish(way, to_chip, behind, part):
        @pl.when(behind)
        def _():
            line_copy(way, to_chip, part).wait_recv()
            acc[way, parts[part], :] += recv_buf[way, to_chip, parts[part], :].astype(F32)

        send_buf[way, to_chip, part * cut : (part + 1) * cut, :] = acc[
            way, part * cut : (part + 1) * cut, :
        ].astype(BF16)
        if part == 1:
            tail = acc[way, 2 * cut :, :]
            four = [tail[at * lane_blocks : (at + 1) * lane_blocks] for at in range(4)]
            high, kept = (four[at].astype(BF16).astype(F32) for at in (0, 2))
            send_buf[way, to_chip, 2 * cut :, :] = jnp.concatenate(
                [high, four[0] + four[1] - high, kept, four[2] + four[3] - kept], axis=0
            ).astype(BF16)
        line_copy(way, to_chip, part).start()

    loads[6].wait()
    for span in spans:
        flip_sat(0, 0, span)
    for way in range(2):
        to_chip, wanted, _ = step_of(way, 0)

        @pl.when(wanted)
        def _():
            add_sat(way, 0, to_chip, 0)

    list_copy.wait_recv()
    for copy, span in zip(tile_copies, spans):
        copy.wait_recv()
        flip_sat(1, 0, span)

    keep = pltpu.make_async_copy(anomaly_buf, anomaly, load.at[8])

    own_step = jnp.where(jnp.logical_and(has_low, has_high), 0, chips - 2)

    def own_terms():
        for part in range(2):
            for side in range(2):
                add_sat(2, part, chip, side)
        loads[7].wait()
        ensemble = members_buf[...].astype(F32)
        state_mean = jnp.mean(ensemble, axis=0, keepdims=True)
        anomaly_buf[...] = (ensemble - state_mean).astype(BF16)
        keep.start()
        centre[...] = jnp.broadcast_to(state_mean, centre.shape)

    def step_body(step, carry):
        for part in range(2):
            if part == 1:
                @pl.when(step == 0)
                def _():
                    for side in range(2):
                        for span in spans:
                            flip_sat(side, 1, span)

            for way in range(2):
                to_chip, wanted, behind = step_of(way, step)

                @pl.when(wanted)
                def _():
                    @pl.when(jnp.logical_or(step > 0, part == 1))
                    def _():
                        add_sat(way, part, to_chip, 0)

                    add_sat(way, part, to_chip, 1)

                    @pl.when(to_chip == near)
                    def _():
                        if part == 0:
                            conv_ready()
                        add_conv(way, part, 2 * to_chip + core, (0, 1))

            for way in range(2):
                to_chip, wanted, behind = step_of(way, step)

                @pl.when(wanted)
                def _():
                    finish(way, to_chip, behind, part)

        @pl.when(step == own_step)
        def _():
            own_terms()

        if chips > 2:
            @pl.when(step == chips - 3)
            def _():
                relay()

        return carry

    if chips == 2:
        relay()

    lax.fori_loop(0, chips - 1, step_body, 0)

    @pl.when(jnp.logical_not(has_near))
    def _():
        conv_ready()

    for part in range(2):
        add_conv(2, part, block, (0, 1))

    @pl.when(outer)
    def _():
        @pl.when(has_north)
        def _():
            far_south.wait_recv()

        @pl.when(has_south)
        def _():
            far_north.wait_recv()

        for part in range(2):
            add_conv(2, part, block, (2,))

    for part in range(2):
        for way, behind in enumerate((has_low, has_high)):
            @pl.when(behind)
            def _():
                line_copy(way, chip, part).wait_recv()
                acc[2, parts[part], :] += recv_buf[way, chip, parts[part], :].astype(F32)

        out[parts[part], :] = acc[2, parts[part], :]

    keep.wait()
    for copy in tile_copies:
        copy.wait_send()
    list_copy.wait_send()
    to_side.wait_send()

    @pl.when(outer)
    def _():
        around.wait_send()

        @pl.when(has_north)
        def _():
            far_north.wait_send()

        @pl.when(has_south)
        def _():
            far_south.wait_send()

    @pl.when(has_north)
    def _():
        to_north.wait_send()
        relays[0].wait_send()

    @pl.when(has_south)
    def _():
        to_south.wait_send()
        relays[1].wait_send()

    def drain(step, carry):
        for way in range(2):
            to_chip, wanted, _ = step_of(way, step)

            @pl.when(wanted)
            def _():
                for part in range(2):
                    line_copy(way, to_chip, part).wait_send()
        return carry

    lax.fori_loop(0, chips - 1, drain, 0)


def analyse_kernel(
    packed, state_mean, spread, out, anomaly_buf, out_buf, y, u, w, e, f, h, t, load, store
):
    members = spread.shape[0]
    fetch = pltpu.make_async_copy(spread, anomaly_buf, load)
    fetch.start()
    half, lane_blocks = members // 2, members // LANES
    blocks = [packed[at * half : (at + 1) * half] for at in range(lane_blocks)]
    cross = jnp.concatenate(blocks[: lane_blocks // 2], axis=1)
    field = jnp.concatenate(blocks[lane_blocks // 2 :], axis=1)
    tail = packed[lane_blocks * half :]

    def tail_row(first, count):
        at = [first * lane_blocks + each for each in range(count)]
        return jnp.concatenate(
            [tail[each : each + 1] + tail[each + lane_blocks : each + lane_blocks + 1] for each in at], axis=1
        )

    drive = tail_row(0, lane_blocks)
    diagonal = tail_row(2, lane_blocks // 2)
    row, col = iota((half, half), 0), iota((half, half), 1)
    on = row == col
    turned = field.T
    first = jnp.where(row < col, field, turned) + jnp.where(on, members - 1.0, 0.0)
    second = jnp.where(on, diagonal + (members - 1.0), jnp.where(row > col, field, turned))
    lone = diagonal + (members - 1.0)
    apart = jnp.where(on, 0.0, field)
    kept = field + (members - 1.0)
    squares = 2.0 * (apart * apart + cross * cross) + jnp.where(on, kept * kept, 0.0)
    square_sum = jnp.sum(
        jnp.sum(squares, axis=0, keepdims=True) + lone * lone, axis=1, keepdims=True
    )
    scale = jnp.sqrt(square_sum)
    shrink = 1.0 / scale
    upper_right = cross * shrink
    y[:half, :half] = (first * shrink).astype(BF16)
    y[half:, half:] = (second * shrink).astype(BF16)
    y[:half, half:] = upper_right.astype(BF16)
    y[half:, :half] = upper_right.T.astype(BF16)

    bands = [slice(at * half, (at + 1) * half) for at in range(2)]
    for band in bands:
        own = y[band, :].astype(F32)
        square = dot(y[band, :], y[...])
        u[band, :] = (1.5 * own - 0.5 * square).astype(BF16)
        w[band, :] = (0.25 * square - 1.5 * own).astype(BF16)
    for band in bands:
        product = dot(u[band, :], w[...])
        e[band, :] = (
            -0.75 * y[band, :].astype(F32) - 1.125 * u[band, :].astype(F32) - 0.5 * product
        ).astype(BF16)
    for band in bands:
        f[band, :] = (2.25 * y[band, :].astype(F32) + dot(y[band, :], e[...])).astype(BF16)
        h[band, :] = (4.5 * e[band, :].astype(F32) + dot(e[band, :], e[...])).astype(BF16)
    def times(vector, matrix):
        high = vector.astype(BF16)
        low = (vector - high.astype(F32)).astype(BF16)
        place = iota((16, members), 0)
        both = jnp.where(place == 0, high.astype(F32), jnp.where(place == 1, low.astype(F32), 0.0))
        product = dot(both.astype(BF16), matrix[...])
        return product[0:1] + product[1:2]

    for band in bands:
        product = dot(f[band, :], h[...])
        t[band, :] = (
            1.5 * e[band, :].astype(F32) - 2.53125 * f[band, :].astype(F32) - 0.5 * product
        ).astype(BF16)
    push = 3.375 * drive + times(drive, t)
    mean_weight = (3.375 * push + times(push, t)) * shrink
    gain = jnp.sqrt((members - 1.0) * shrink)
    fetch.wait()
    part = members // STORES
    stores = [
        pltpu.make_async_copy(
            out_buf.at[pl.ds(at * part, part)], out.at[0, 0, pl.ds(at * part, part)], store.at[at]
        )
        for at in range(STORES)
    ]
    for at, copy in enumerate(stores):
        band = slice(at * part, (at + 1) * part)
        one = iota((part, members), 0) + at * part == iota((part, members), 1)
        root = t[band, :].astype(F32) + jnp.where(one, 3.375, 0.0)
        transform = (gain * root + mean_weight).astype(BF16)
        out_buf[band, :] = dot(transform, anomaly_buf[...]) + state_mean[0:1]
        copy.start()
    for copy in stores:
        copy.wait()


def shards(
    n_lat, n_lon,
    background, conv_pert, conv_misfit, conv_column, sat_pert, sat_misfit, sat_rows, sat_targets,
):
    members, cells = background.shape[2:]
    tiles, tile_obs = sat_pert.shape[1:3]
    conv_obs = conv_pert.shape[2]
    rows, chips, half = tiles * tile_obs, n_lon // 2, members // 2
    vmem = pl.BlockSpec(memory_space=pltpu.VMEM)
    lanes_long = members // LANES * half + EXTRA
    hbm = pl.BlockSpec(memory_space=pltpu.HBM)
    packed, anomaly, state_mean = pl.pallas_call(
        functools.partial(gather_kernel, n_lat, n_lon),
        out_shape=(
            jax.ShapeDtypeStruct((lanes_long, LANES), F32),
            jax.ShapeDtypeStruct((members, cells), BF16),
            jax.ShapeDtypeStruct((8, cells), F32),
        ),
        in_specs=[hbm] * 8,
        out_specs=(vmem, hbm, vmem),
        scratch_shapes=[
            pltpu.VMEM((members, cells), BF16),
            pltpu.VMEM((members, cells), BF16),
            pltpu.VMEM((1, 1, conv_obs), BF16),
            pltpu.VMEM((1, 1, conv_obs), jnp.int32),
            pltpu.VMEM((1, tiles, tile_obs), BF16),
            pltpu.VMEM((1, tiles), jnp.int32),
            pltpu.VMEM((1, 2, tiles), jnp.int32),
            pltpu.VMEM((2, rows, members), BF16),
            pltpu.VMEM((2, EXTRA, rows), BF16),
            pltpu.VMEM((3, 3, conv_obs + EXTRA, members), BF16),
            pltpu.VMEM((2, members, rows), BF16),
            pltpu.VMEM((members, 6 * conv_obs), BF16),
            pltpu.VMEM((3, lanes_long, LANES), F32),
            pltpu.VMEM((2, chips, lanes_long, LANES), BF16),
            pltpu.VMEM((2, chips, lanes_long, LANES), BF16),
            pltpu.SemaphoreType.DMA((9,)),
            pltpu.SemaphoreType.DMA((3,)),
            pltpu.SemaphoreType.DMA((3,)),
            pltpu.SemaphoreType.DMA((8,)),
            pltpu.SemaphoreType.DMA((8,)),
            pltpu.SemaphoreType.DMA((2, chips, 2)),
            pltpu.SemaphoreType.DMA((2, chips, 2)),
        ],
        compiler_params=pltpu.CompilerParams(
            collective_id=0, has_side_effects=True, vmem_limit_bytes=64 * 1024 * 1024
        ),
        cost_estimate=pl.CostEstimate(
            flops=2 * (chips * 2 * rows + 9 * conv_obs) * members * members,
            bytes_accessed=4 * rows * members, transcendentals=0,
        ),
        name="gather_grams",
    )(
        background, conv_pert, conv_misfit, conv_column, sat_pert.reshape(rows, members), sat_misfit, sat_rows,
        jnp.swapaxes(sat_targets, 1, 2),
    )
    return pl.pallas_call(
        analyse_kernel,
        out_shape=jax.ShapeDtypeStruct((1, 1, members, cells), F32),
        in_specs=[vmem, vmem, hbm],
        out_specs=hbm,
        scratch_shapes=[
            pltpu.VMEM((members, cells), BF16),
            pltpu.VMEM((members, cells), F32),
            *[pltpu.VMEM((members, members), BF16)] * 7,
            pltpu.SemaphoreType.DMA,
            pltpu.SemaphoreType.DMA((STORES,)),
        ],
        compiler_params=pltpu.CompilerParams(vmem_limit_bytes=64 * 1024 * 1024),
        cost_estimate=pl.CostEstimate(
            flops=14 * members * members * members, bytes_accessed=6 * members * cells, transcendentals=0
        ),
        name="analyse",
    )(packed, state_mean, anomaly)


def solution(mesh):
    placed = (
        P("lat", "lon", None, None),
        P("lat", "lon", None, None),
        P("lat", "lon", None),
        P("lat", "lon", None),
        P("lat", "lon", None, None),
        P("lat", "lon", None),
        P("lat", "lon"),
        P("lat", "lon", None),
    )
    return jax.shard_map(
        functools.partial(shards, mesh.shape["lat"], mesh.shape["lon"]),
        mesh=mesh, in_specs=placed, out_specs=P("lat", "lon", None, None), check_vma=False,
    )
```
